32 devices in a mesh: cell: 1, section: 32 (over z, y, x, core).
Axes of the slice: x: 2, y: 2, z: 4, core: 2. Of those that a mesh axis runs over, the one named last changes fastest.
Arguments:
- hidden: bfloat16 [12288, 8192], P(('cell', 'section')), may hold values from -6 to 6
- norm_gain: bfloat16 [8192], replicated, may hold values from 0.25 to 1.75
- queries: bfloat16 [12288, 1024], P(('cell', 'section')), may hold values from -110 to 110
- w_kv: bfloat16 [8192, 256], replicated, may hold values from -0.0625 to 0.0625
- plan: int32 [32], P('cell'), may hold values from 0 to 31, each once
- prompt_spans: int32 [4], P('cell'), may hold values from 1 to 16, 32 in all
- placement: int32 [1536, 2], P('cell'), may hold values from 0 to 47, as said below
Outputs:
- context: bfloat16 [12288, 1024], P(('cell', 'section'))
- cache_out: bfloat16 [1536, 8, 256], P(('cell', 'section'))
The draws below stay inside these ranges and needn't reach their ends.
Inputs may be any that keep to these rules, and one draw needn't show every extreme that they name: plan[g] is the span held by group g; every span is held by one group. `prompt_spans`: the lengths sum to 32; one prompt has exactly 16 spans. placement[b] = (owner, slot) of block b. The 48 blocks of one span go to 24 owners, exactly 2 to each; every owner receives exactly 48 blocks, one in each of its slots 0 to 47.
All inputs are finite; a program needn't handle non-finite values.
Results may differ from the reference program's by a relative error of at most 0.0055.
The reference program's roundings to bfloat16 on the way (of `normed`, `keys_values`, `scaled_queries` and `rounded_weights`) count: a program that leaves them out, or rounds other values in their place, can miss the bound.
Values may be sent and summed in bfloat16 or wider, within the bound.
No kernel may reach another device: no remote copies, remote signals or barrier semaphores. Data moves between devices by JAX's collectives and lax.ppermute only.
A program may use at most 128 MiB of HBM per device.

```python
import math
import jax
import jax.numpy as jnp
import numpy as np
from jax import lax

D = 8192
HD = 128
HQ = 8
SPAN = 384
BLK = 8
PMAX = 16
SPANS = 32
TOKENS = 12288
PROMPTS = 4
BLOCKS = 48
CAP = 2


def draw_queries(key, part):
    key = jax.random.fold_in(key, 11)
    row_key, value_key = jax.random.split(key)
    row_scale = jnp.exp(jax.random.uniform(row_key, (TOKENS, 1), jnp.float32, math.log(0.7), math.log(1.4)))
    values = jax.random.truncated_normal(value_key, -5.0, 5.0, (TOKENS, HQ * HD), jnp.float32)
    return (values * row_scale).astype(jnp.bfloat16)


def draw_placement(key, part):
    key = jax.random.fold_in(key, 5)
    first_key, second_key, third_key = jax.random.split(key, 3)
    sigma = jax.random.permutation(first_key, SPANS)
    shifted = jax.random.permutation(second_key, SPANS)
    owner_groups = BLOCKS // CAP
    span_index = jnp.arange(SPANS, dtype=jnp.int32)[:, None, None]
    group_index = jnp.arange(owner_groups, dtype=jnp.int32)[None, :, None]
    within = jnp.arange(CAP, dtype=jnp.int32)[None, None, :]
    owners = sigma[(shifted[span_index] + group_index) % SPANS] + 0 * within
    slots = group_index * CAP + within + 0 * span_index
    orders = jax.vmap(lambda single: jax.random.permutation(single, BLOCKS))(jax.random.split(third_key, SPANS))
    block_ids = (jnp.arange(SPANS, dtype=jnp.int32)[:, None] * BLOCKS + orders).reshape(-1)
    pairs = jnp.stack([owners.reshape(-1), slots.reshape(-1)], axis=1).astype(jnp.int32)
    return jnp.zeros((SPANS * BLOCKS, 2), jnp.int32).at[block_ids].set(pairs)


def block_levels(own_key, dims, shards, least, high):
    def one(position, shards_of):
        draws = jax.random.uniform(jax.random.fold_in(jax.random.fold_in(own_key, 6), position), (shards_of,), jnp.float32, least / len(shards), high / len(shards))
        return jnp.repeat(jnp.exp(draws), dims[position] // shards_of).reshape((-1,) + (1,) * (len(dims) - position - 1))

    gain = one(*shards[0])
    for cut in shards[1:]:
        gain = gain * one(*cut)
    return gain


def split_up(number_of, total, limit, lean):
    portions = [(1 << 20) // math.isqrt(standing ** lean) + 1 for standing in range(2, number_of + 1)]
    spare, holding = total - limit - (number_of - 1), [1] * (number_of - 1)
    while spare > 0:
        movable = [i for i in range(number_of - 1) if holding[i] < limit]
        mass, remaining = sum([portions[i] for i in movable]), spare
        for i in movable:
            more = min(limit - holding[i], max(1, remaining * portions[i] // mass), spare)
            holding[i] = holding[i] + more
            spare = spare - more
    return np.array([limit] + holding)


def uneven_parts(rng, number_of, total, bound, lean):
    if number_of == 2:
        one = jax.random.randint(rng, (), max(1, total - bound), min(bound, total - 1) + 1)
        return jnp.stack([one, total - one])
    sizes = jnp.asarray(split_up(number_of, total, bound, lean), jnp.int32)
    couples = (number_of - 1) // 2
    giver, sink = sizes[1:1 + 2 * couples:2], sizes[2:2 + 2 * couples:2]
    margin = jnp.minimum(giver - 1, bound - sink)
    passed = jax.random.randint(jax.random.fold_in(rng, 1), (couples,), 0, 1 << 20) % (margin + 1)
    sizes = sizes.at[1:1 + 2 * couples:2].set(giver - passed).at[2:2 + 2 * couples:2].set(sink + passed)
    return sizes[jax.random.permutation(jax.random.fold_in(rng, 2), number_of)]


def gaussian(stream_key, dims, spread, limit, cuts=(), held_as=jnp.bfloat16):
    array = jax.random.normal(stream_key, dims, jnp.float32) * spread
    if len(cuts) > 0:
        array = block_levels(stream_key, dims, cuts, -0.22, 0.18) * array
    return jnp.clip(array, min=-limit, max=limit).astype(held_as)


def setup_inputs(seed: int = 0, part: int = 0) -> dict:
    key_of = jax.random.split(jax.random.key(seed), 8)
    own_keys = jax.random.split(jax.random.fold_in(key_of[7], part), 8)
    return {
        "hidden": gaussian(own_keys[0], (TOKENS, D), 1.0, 6.0, ((0, 32),)),
        "norm_gain": jnp.clip(1.0 + 0.15 * jax.random.normal(key_of[1], (D,), jnp.float32), 0.25, 1.75).astype(jnp.bfloat16),
        "queries": draw_queries(jax.random.fold_in(jax.random.fold_in(key_of[7], part), 71), part),
        "w_kv": gaussian(key_of[3], (D, 2 * HD), D ** -0.5, 0.0625),
        "plan": jax.random.permutation(own_keys[4], SPANS).astype(jnp.int32),
        "prompt_spans": uneven_parts(own_keys[5], PROMPTS, SPANS, PMAX, 1).astype(jnp.int32),
        "placement": draw_placement(jax.random.fold_in(jax.random.fold_in(key_of[7], part), 71), part),
    }


def span_layout(prompt_spans, group_total):
    prompt_end = jnp.cumsum(prompt_spans).astype(jnp.int32)
    prompt_start = prompt_end - prompt_spans
    span_ids = jnp.arange(group_total, dtype=jnp.int32)
    owning_prompt = lax.optimization_barrier(jnp.sum((span_ids[:, None] >= prompt_end[None, :]).astype(jnp.int32), axis=1))
    member = (owning_prompt[:, None] == jnp.arange(prompt_spans.shape[0], dtype=jnp.int32)[None, :]).astype(jnp.int32)
    first_span = lax.optimization_barrier(jnp.sum(member * prompt_start[None, :], axis=1))
    return (first_span, span_ids - first_span)

def rotary(values, positions):
    half_size = values.shape[-1] // 2
    frequency = 500000.0 ** (-jnp.arange(half_size, dtype=jnp.float32) * 2.0 / values.shape[-1])
    angles = positions.astype(jnp.float32).reshape(positions.shape + (1,) * (values.ndim - 1)) * frequency
    cosine = jnp.cos(angles)
    sine_part = jnp.sin(angles)
    first_half = values[..., :half_size]
    second_half = values[..., half_size:]
    return jnp.concatenate([first_half * cosine - second_half * sine_part, second_half * cosine + first_half * sine_part], axis=-1)

def reference(hidden, norm_gain, queries, w_kv, plan, prompt_spans, placement):
    first_span, span_depth = span_layout(prompt_spans, SPANS)
    row_index = jnp.arange(SPAN, dtype=jnp.int32)
    positions = (span_depth[plan][:, None] * SPAN + row_index[None, :]).reshape(-1)
    floats = hidden.astype(jnp.float32)
    mean_square = lax.optimization_barrier(jnp.mean(floats * floats, axis=-1, keepdims=True))
    normed = (floats * lax.rsqrt(mean_square + 1e-05) * norm_gain.astype(jnp.float32)).astype(jnp.bfloat16)
    projected = jnp.dot(normed, w_kv, preferred_element_type=jnp.float32)
    rotated_keys = rotary(projected[:, :HD], positions)
    keys_values = jnp.concatenate([rotated_keys, projected[:, HD:]], axis=1).astype(jnp.bfloat16)
    rotated = rotary(queries.astype(jnp.float32).reshape(TOKENS, HQ, HD), positions)
    scaled_queries = (rotated * HD ** (-0.5)).astype(jnp.bfloat16)
    inverse = jnp.zeros((SPANS,), jnp.int32).at[plan].set(jnp.arange(SPANS, dtype=jnp.int32))
    blocks_kv = keys_values.reshape(SPANS, SPAN, 2 * HD)
    blocks_query = scaled_queries.reshape(SPANS, SPAN, HQ, HD)
    lag_steps = jnp.arange(PMAX, dtype=jnp.int32)

    def per_group(group_index):
        own_span = plan[group_index]
        source_span = own_span - lag_steps
        in_prompt = source_span >= first_span[own_span]
        source_group = inverse[jnp.maximum(source_span, 0)]
        key_blocks = blocks_kv[source_group]
        key_part = key_blocks[:, :, :HD].astype(jnp.float32)
        value_part = key_blocks[:, :, HD:].astype(jnp.float32)
        query_block = blocks_query[group_index].astype(jnp.float32)
        scores = jnp.einsum('qhd,pkd->qhpk', query_block, key_part)
        causal = row_index[None, None, None, :] <= row_index[:, None, None, None]
        allowed = in_prompt[None, None, :, None] & ((lag_steps[None, None, :, None] > 0) | causal)
        masked = jnp.where(allowed, scores, -1e+30)
        row_max = lax.optimization_barrier(jnp.max(masked, axis=(2, 3), keepdims=True))
        weights_exp = jnp.where(allowed, jnp.exp(masked - row_max), 0.0)
        denominator = lax.optimization_barrier(jnp.sum(weights_exp, axis=(2, 3)))
        rounded_weights = lax.optimization_barrier(weights_exp.astype(jnp.bfloat16)).astype(jnp.float32)
        attended = jnp.einsum('qhpk,pkd->qhd', rounded_weights, value_part) / denominator[..., None]
        return attended.astype(jnp.bfloat16).reshape(SPAN, HQ * HD)
    context = lax.map(per_group, jnp.arange(SPANS, dtype=jnp.int32)).reshape(TOKENS, HQ * HD)
    span_blocks = blocks_kv[inverse].reshape(SPANS * BLOCKS, BLK, 2 * HD)
    target = placement[:, 0] * BLOCKS + placement[:, 1]
    cache_out = jnp.zeros((SPANS * BLOCKS, BLK, 2 * HD), jnp.bfloat16).at[target].set(span_blocks)
    return (context, cache_out)
```

```python
import functools

import jax
import jax.numpy as jnp
import numpy as np
from jax import lax
from jax.experimental import pallas as pl
from jax.experimental.pallas import tpu as pltpu
from jax.sharding import PartitionSpec as P

BLK = 8
THETA = 500000.0
EPS = 1e-05
ONES = 16
NEG = -1e30
VMEM_LIMIT = 56 * 1024 * 1024
SMEM_SPEC = pl.BlockSpec(memory_space=pltpu.SMEM)
VMEM_SPEC = pl.BlockSpec(memory_space=pltpu.VMEM)
ANY_SPEC = pl.BlockSpec(memory_space=pl.ANY)


def rotary_tables(rows, head, spans):
    half = head // 2
    freq = THETA ** (-np.arange(half, dtype=np.float64) * 2.0 / head)
    freq = np.concatenate([freq, freq])
    inner = np.arange(rows, dtype=np.float64)[:, None] * freq
    outer = np.arange(spans, dtype=np.float64)[:, None] * rows * freq
    as32 = lambda a: jnp.asarray(a.astype(np.float32))
    return (as32(np.cos(inner)), as32(np.sin(inner)), as32(np.cos(outer)), as32(np.sin(outer)))


def own_place(prompt_ref, own_span):
    first = jnp.int32(0)
    end = jnp.int32(0)
    for p in range(prompt_ref.shape[0]):
        end = end + prompt_ref[p]
        first = jnp.where(own_span >= end, end, first)
    return first, own_span - first


def angles(depth, cos_in, sin_in, cos_out, sin_out):
    head = cos_in.shape[1]
    c0, s0 = cos_out[pl.ds(depth, 1), :], sin_out[pl.ds(depth, 1), :]
    c, s = cos_in[...], sin_in[...]
    cosine = c0 * c - s0 * s
    sine = s0 * c + c0 * s
    lane = lax.broadcasted_iota(jnp.int32, sine.shape, 1)
    return cosine, jnp.where(lane < head // 2, -sine, sine)


def rotate(x, cosine, sine):
    half = x.shape[1] // 2
    return x * cosine + jnp.concatenate([x[:, half:], x[:, :half]], axis=1) * sine


def project_kernel(plan_ref, prompt_ref, me_ref, hid_hbm, gain_ref, w_hbm, ci, si, co, so, kv_ref,
                   hid, w, acc, hsem, wsem, *, row_tiles, k_tiles):
    rows, width = hid.shape
    head = kv_ref.shape[1] // 2
    rt, kt = rows // row_tiles, width // k_tiles
    hcopy = [pltpu.make_async_copy(hid_hbm.at[pl.ds(i * rt, rt)], hid.at[pl.ds(i * rt, rt)], hsem.at[i])
             for i in range(row_tiles)]
    wcopy = [pltpu.make_async_copy(w_hbm.at[pl.ds(i * kt, kt)], w.at[pl.ds(i * kt, kt)], wsem.at[i])
             for i in range(k_tiles)]
    for cp in hcopy + wcopy:
        cp.start()
    own_span = plan_ref[me_ref[0]]
    _, depth = own_place(prompt_ref, own_span)
    scales = []
    for i in range(row_tiles):
        hcopy[i].wait()
        total = jnp.zeros((rt, 128), jnp.float32)
        for j in range(width // 128):
            x = hid[i * rt:(i + 1) * rt, j * 128:(j + 1) * 128].astype(jnp.float32)
            total = total + x * x
        mean = jnp.sum(total, axis=1, keepdims=True) * (1.0 / width)
        scales.append(lax.rsqrt(mean + EPS))
    scale = jnp.concatenate(scales, axis=0)
    for j in range(k_tiles):
        cols = slice(j * kt, (j + 1) * kt)
        x = hid[:, cols].astype(jnp.float32)
        normed = (x * scale * gain_ref[:, cols].astype(jnp.float32)).astype(jnp.bfloat16)
        wcopy[j].wait()
        part = jnp.dot(normed, w[cols, :], preferred_element_type=jnp.float32)
        if j == 0:
            acc[...] = part
        else:
            acc[...] += part
    cosine, sine = angles(depth, ci, si, co, so)
    kv_ref[:, :head] = rotate(acc[:, :head], cosine, sine).astype(jnp.bfloat16)
    kv_ref[:, head:] = acc[:, head:].astype(jnp.bfloat16)


def project(plan, prompt_spans, me, hidden, gain, w_kv, tables):
    rows, width = hidden.shape
    row_tiles, k_tiles = 6, 16
    return pl.pallas_call(
        functools.partial(project_kernel, row_tiles=row_tiles, k_tiles=k_tiles),
        out_shape=jax.ShapeDtypeStruct((rows, w_kv.shape[1]), jnp.bfloat16),
        in_specs=[SMEM_SPEC] * 3 + [ANY_SPEC, VMEM_SPEC, ANY_SPEC] + [VMEM_SPEC] * 4,
        out_specs=VMEM_SPEC,
        scratch_shapes=[
            pltpu.VMEM((rows, width), jnp.bfloat16),
            pltpu.VMEM(w_kv.shape, jnp.bfloat16),
            pltpu.VMEM((rows, w_kv.shape[1]), jnp.float32),
            pltpu.SemaphoreType.DMA((row_tiles,)),
            pltpu.SemaphoreType.DMA((k_tiles,)),
        ],
        compiler_params=pltpu.CompilerParams(vmem_limit_bytes=VMEM_LIMIT),
        name="project",
    )(plan, prompt_spans, me, hidden, gain, w_kv, *tables)


def softmax_step(keys, values_t, q_ref, chunk, acc, row_max, masked):
    columns = q_ref.shape[1]
    count = columns // chunk
    scores = lambda c: jnp.dot(keys, q_ref[:, c * chunk:(c + 1) * chunk], preferred_element_type=jnp.float32)
    after = scores(0)
    for c in range(count):
        cols = slice(c * chunk, (c + 1) * chunk)
        s = after
        if c + 1 < count:
            after = scores(c + 1)
        if masked is not None:
            s = masked(s)
        old = row_max[:, cols]
        new = jnp.maximum(old, jnp.max(s, axis=0, keepdims=True))
        factor = jnp.exp(old - new)
        weights = jnp.exp(s - new).astype(jnp.bfloat16)
        row_max[:, cols] = new
        acc[:, cols] = acc[:, cols] * factor + jnp.dot(values_t, weights, preferred_element_type=jnp.float32)


def queries_kernel(plan_ref, prompt_ref, me_ref, place_ref, q_ref, kv_ref, ci, si, co, so,
                   qt_ref, acc, row_max, sel_ref, vt):
    rows = q_ref.shape[0]
    head = ci.shape[1]
    heads = q_ref.shape[1] // head
    me = me_ref[0]
    own_span = plan_ref[me]
    _, depth = own_place(prompt_ref, own_span)
    cosine, sine = angles(depth, ci, si, co, so)
    for h in range(heads):
        x = q_ref[:, h * head:(h + 1) * head].astype(jnp.float32)
        x = (rotate(x, cosine, sine) * head ** (-0.5)).astype(jnp.bfloat16)
        qt_ref[:, h * rows:(h + 1) * rows] = x.T
    slots = sel_ref.shape[0]
    blocks = place_ref.shape[1]
    mine = (place_ref[0:1, :] == me) & (
        place_ref[1:2, :] == lax.broadcasted_iota(jnp.int32, (slots, blocks), 0))
    block_id = lax.broadcasted_iota(jnp.int32, (slots, blocks), 1).astype(jnp.float32)
    sel_ref[...] = jnp.sum(jnp.where(mine, block_id, 0.0), axis=1, keepdims=True).astype(jnp.int32)
    acc[...] = jnp.zeros_like(acc)
    row_max[...] = jnp.full_like(row_max, NEG)
    vt[head:, :] = jnp.ones((ONES, rows), jnp.bfloat16)
    vt[:head, :] = kv_ref[:, head:].T

    def causal(s):
        key = lax.broadcasted_iota(jnp.int32, s.shape, 0)
        row = lax.broadcasted_iota(jnp.int32, s.shape, 1)
        return jnp.where(key <= row, s, NEG)

    softmax_step(kv_ref[:, :head], vt[...], qt_ref, rows, acc, row_max, causal)


def prepare(plan, prompt_spans, me, place, queries, kv, tables):
    rows = queries.shape[0]
    head = kv.shape[1] // 2
    columns = rows * (queries.shape[1] // head)
    return pl.pallas_call(
        queries_kernel,
        out_shape=(
            jax.ShapeDtypeStruct((head, columns), jnp.bfloat16),
            jax.ShapeDtypeStruct((head + ONES, columns), jnp.float32),
            jax.ShapeDtypeStruct((1, columns), jnp.float32),
            jax.ShapeDtypeStruct((rows // BLK, 1), jnp.int32),
        ),
        in_specs=[SMEM_SPEC] * 3 + [VMEM_SPEC] * 7,
        out_specs=(VMEM_SPEC,) * 4,
        scratch_shapes=[pltpu.VMEM((head + ONES, rows), jnp.bfloat16)],
        compiler_params=pltpu.CompilerParams(vmem_limit_bytes=VMEM_LIMIT),
        name="prepare",
    )(plan, prompt_spans, me, place, queries, kv, *tables)


def finish_kernel(plan_ref, prompt_ref, me_ref, src_ref, sel_ref, qt_ref, acc_in, max_in, *rest, pieces):
    refs = rest[:pieces]
    ctx_ref, cache_ref, kv, acc, row_max, vt, sem = rest[pieces:]
    head, columns = qt_ref.shape
    rows = refs[0].shape[0]
    me = me_ref[0]

    def copy(j):
        span = plan_ref[src_ref[me * pieces + j]]
        return pltpu.make_async_copy(refs[j], kv.at[pl.ds(pl.multiple_of(span * rows, rows), rows)], sem)

    for j in range(pieces):
        copy(j).start()
    own_span = plan_ref[me]
    first, _ = own_place(prompt_ref, own_span)
    acc[...] = acc_in[...]
    row_max[...] = max_in[...]
    vt[head:, :] = jnp.ones((ONES, 2 * rows), jnp.bfloat16)
    for j in range(pieces):
        copy(j).wait()

    def visit(span, count):
        base = pl.multiple_of(span * rows, rows)
        vt[:head, :count * rows] = kv[pl.ds(base, count * rows), head:].T
        softmax_step(kv[pl.ds(base, count * rows), :head], vt[:, :count * rows], qt_ref, 512, acc, row_max, None)

    odd = (own_span - first) % 2

    @pl.when(odd == 1)
    def _():
        visit(first, 1)

    @pl.loop(0, (own_span - first) // 2)
    def _(i):
        visit(first + odd + 2 * i, 2)

    for h in range(columns // rows):
        cols = slice(h * rows, (h + 1) * rows)
        out = acc[:head, cols] / acc[head:head + 1, cols]
        ctx_ref[:, h * head:(h + 1) * head] = out.astype(jnp.bfloat16).T

    @pl.loop(0, cache_ref.shape[0])
    def _(slot):
        block = sel_ref[slot, 0]
        pair = kv[pl.ds(pl.multiple_of((block // 2) * (2 * BLK), 2 * BLK), 2 * BLK), :].astype(jnp.float32)
        cache_ref[slot] = jnp.where(block % 2 == 1, pair[BLK:], pair[:BLK]).astype(jnp.bfloat16)


def finish(plan, prompt_spans, me, sources, sel, qt, acc, row_max, pieces):
    head, columns = qt.shape
    rows, both = pieces[0].shape
    heads = columns // rows
    n = len(pieces)
    return pl.pallas_call(
        functools.partial(finish_kernel, pieces=n),
        out_shape=(
            jax.ShapeDtypeStruct((rows, heads * head), jnp.bfloat16),
            jax.ShapeDtypeStruct((rows // BLK, BLK, both), jnp.bfloat16),
        ),
        in_specs=[SMEM_SPEC] * 5 + [VMEM_SPEC] * 3 + [ANY_SPEC] * n,
        out_specs=(VMEM_SPEC,) * 2,
        scratch_shapes=[
            pltpu.VMEM((n * rows, both), jnp.bfloat16),
            pltpu.VMEM(acc.shape, jnp.float32),
            pltpu.VMEM(row_max.shape, jnp.float32),
            pltpu.VMEM((head + ONES, 2 * rows), jnp.bfloat16),
            pltpu.SemaphoreType.DMA,
        ],
        compiler_params=pltpu.CompilerParams(vmem_limit_bytes=VMEM_LIMIT),
        name="finish",
    )(plan, prompt_spans, me, sources, sel, qt, acc, row_max, *pieces)


class Routes:
    def __init__(self, n):
        self.n = n
        self.lines = n // 8
        order = [0] + list(range(1, self.lines, 2)) + list(range(2, self.lines, 2))[::-1]
        following = {a: order[(i + 1) % self.lines] for i, a in enumerate(order)}
        preceding = {b: a for a, b in following.items()}
        self.ahead = [self.at(following[l], y, x, c) for l, y, x, c in self.all()]
        self.back = [self.at(preceding[l], y, x, c) for l, y, x, c in self.all()]
        self.flip_a = [self.at(l, y, 1 - x, c) if c == 0 else self.at(l, 1 - y, x, c) for l, y, x, c in self.all()]
        self.flip_b = [self.at(l, y, 1 - x, c) if c == 1 else self.at(l, 1 - y, x, c) for l, y, x, c in self.all()]
        self.core = [self.at(l, y, x, 1 - c) for l, y, x, c in self.all()]

    def all(self):
        return [(i // 8, (i // 4) % 2, (i // 2) % 2, i % 2) for i in range(self.n)]

    def at(self, line, y, x, core):
        return ((line * 2 + y) * 2 + x) * 2 + core


def send(item, to):
    array, source = item
    moved = [0] * len(to)
    for i, target in enumerate(to):
        moved[target] = source[i]
    return lax.ppermute(array, "section", list(enumerate(to))), moved


def gather(kv, n):
    r = Routes(n)
    own = (kv, list(range(n)))
    lines = [own]
    ahead = back = own
    for step in range(1, r.lines):
        if step % 2 == 1:
            ahead = send(ahead, r.ahead)
            lines.append(ahead)
        else:
            back = send(back, r.back)
            lines.append(back)
    blocks = []
    for block in lines:
        a, b = send(block, r.flip_a), send(block, r.flip_b)
        blocks += [block, a, b, send(a, r.flip_b)]
    blocks += [send(block, r.core) for block in blocks]
    sources = np.array([source for _, source in blocks], np.int32).T
    return [array for array, _ in blocks], sources


def local(hidden, norm_gain, queries, w_kv, plan, prompt_spans, placement):
    n = lax.axis_size("section")
    rows = hidden.shape[0]
    head = w_kv.shape[1] // 2
    me = lax.axis_index("section").astype(jnp.int32).reshape(1)
    tables = rotary_tables(rows, head, n)
    kv = project(plan, prompt_spans, me, hidden, norm_gain.reshape(1, -1), w_kv, tables)
    pieces, sources = gather(kv, n)
    qt, acc, row_max, sel = prepare(plan, prompt_spans, me, placement.T, queries, kv, tables)
    return finish(plan, prompt_spans, me, jnp.asarray(sources.reshape(-1)), sel, qt, acc, row_max, pieces)


def solution(mesh):
    placed = (
        P(("cell", "section"), None),
        P(),
        P(("cell", "section"), None),
        P(),
        P("cell"),
        P("cell"),
        P("cell", None),
    )
    return jax.shard_map(
        local,
        mesh=mesh,
        in_specs=placed,
        out_specs=(P(("cell", "section"), None), P(("cell", "section"), None, None)),
        check_vma=False,
    )
```

```python
import functools

import jax
import jax.numpy as jnp
import numpy as np
from jax import lax
from jax.experimental import pallas as pl
from jax.experimental.pallas import tpu as pltpu
from jax.sharding import PartitionSpec as P

BLK = 8
THETA = 500000.0
EPS = 1e-05
ONES = 16
NEG = -1e30
VMEM_ALL = 56 * 1024 * 1024
VMEM_PART = 24 * 1024 * 1024
SMEM_SPEC = pl.BlockSpec(memory_space=pltpu.SMEM)
VMEM_SPEC = pl.BlockSpec(memory_space=pltpu.VMEM)
ANY_SPEC = pl.BlockSpec(memory_space=pl.ANY)


def rotary_tables(rows, head, spans):
    half = head // 2
    freq = THETA ** (-np.arange(half, dtype=np.float64) * 2.0 / head)
    freq = np.concatenate([freq, freq])
    inner = np.arange(rows, dtype=np.float64)[:, None] * freq
    outer = np.arange(spans, dtype=np.float64)[:, None] * rows * freq
    as32 = lambda a: jnp.asarray(a.astype(np.float32))
    return (as32(np.cos(inner)), as32(np.sin(inner)), as32(np.cos(outer)), as32(np.sin(outer)))


def own_place(prompt_ref, own_span):
    first = jnp.int32(0)
    end = jnp.int32(0)
    for p in range(prompt_ref.shape[0]):
        end = end + prompt_ref[p]
        first = jnp.where(own_span >= end, end, first)
    return first, own_span - first


def angles(depth, cos_in, sin_in, cos_out, sin_out):
    head = cos_in.shape[1]
    c0, s0 = cos_out[pl.ds(depth, 1), :], sin_out[pl.ds(depth, 1), :]
    c, s = cos_in[...], sin_in[...]
    cosine = c0 * c - s0 * s
    sine = s0 * c + c0 * s
    lane = lax.broadcasted_iota(jnp.int32, sine.shape, 1)
    return cosine, jnp.where(lane < head // 2, -sine, sine)


def rotate(x, cosine, sine):
    half = x.shape[1] // 2
    return x * cosine + jnp.concatenate([x[:, half:], x[:, :half]], axis=1) * sine


def project_kernel(plan_ref, prompt_ref, me_ref, hid_hbm, gain_ref, w_hbm, ci, si, co, so, kv_ref,
                   hid, w, scale, gain, hsem, wsem, *, group):
    rows, width = hid.shape
    head = kv_ref.shape[1] // 2
    row_tiles, k_tiles = hsem.shape[0], wsem.shape[0]
    rt, kt = rows // row_tiles, width // k_tiles
    lanes = scale.shape[1]
    hcopy = [pltpu.make_async_copy(hid_hbm.at[pl.ds(i * rt, rt)], hid.at[pl.ds(i * rt, rt)], hsem.at[i])
             for i in range(row_tiles)]
    wcopy = [pltpu.make_async_copy(w_hbm.at[pl.ds(i * kt, kt)], w.at[pl.ds(i * kt, kt)], wsem.at[i])
             for i in range(k_tiles)]
    for cp in hcopy + wcopy:
        cp.start()
    own_span = plan_ref[me_ref[0]]
    _, depth = own_place(prompt_ref, own_span)
    gain[...] = jnp.broadcast_to(gain_ref[...].astype(jnp.float32).reshape(1, width), gain.shape)

    def measure(row):
        sums = [jnp.zeros((group, lanes), jnp.float32)] * 4
        for j in range(width // lanes):
            x = hid[pl.ds(row, group), j * lanes:(j + 1) * lanes].astype(jnp.float32)
            sums[j % 4] = sums[j % 4] + x * x
        total = jnp.sum((sums[0] + sums[1]) + (sums[2] + sums[3]), axis=1, keepdims=True)
        scale[pl.ds(row, group), :] = jnp.broadcast_to(lax.rsqrt(total * (1.0 / width) + EPS), (group, lanes))

    def normalise(row):
        by = scale[pl.ds(row, group), :].reshape(group // 8, 8, lanes)
        for j in range(width // lanes):
            cols = slice(j * lanes, (j + 1) * lanes)
            x = hid[pl.ds(row, group), cols].astype(jnp.float32).reshape(group // 8, 8, lanes)
            hid[pl.ds(row, group), cols] = (x * by * gain[:, cols][None]).reshape(group, lanes).astype(jnp.bfloat16)

    for i in range(row_tiles + 1):
        if i < row_tiles:
            hcopy[i].wait()

        @pl.loop(0, rt // group)
        def _(g):
            if i < row_tiles:
                measure(pl.multiple_of(i * rt + g * group, group))
            if i > 0:
                normalise(pl.multiple_of((i - 1) * rt + g * group, group))

    cosine, sine = angles(depth, ci, si, co, so)
    for cp in wcopy:
        cp.wait()
    projected = jnp.dot(hid[...], w[...], preferred_element_type=jnp.float32)
    kv_ref[:, :head] = rotate(projected[:, :head], cosine, sine).astype(jnp.bfloat16)
    kv_ref[:, head:] = projected[:, head:].astype(jnp.bfloat16)


def project(plan, prompt_spans, me, hidden, gain, w_kv, tables):
    rows, width = hidden.shape
    row_tiles, k_tiles = 6, 4
    return pl.pallas_call(
        functools.partial(project_kernel, group=32),
        out_shape=jax.ShapeDtypeStruct((rows, w_kv.shape[1]), jnp.bfloat16),
        in_specs=[SMEM_SPEC] * 3 + [ANY_SPEC, VMEM_SPEC, ANY_SPEC] + [VMEM_SPEC] * 4,
        out_specs=VMEM_SPEC,
        scratch_shapes=[
            pltpu.VMEM((rows, width), jnp.bfloat16),
            pltpu.VMEM(w_kv.shape, jnp.bfloat16),
            pltpu.VMEM((rows, 128), jnp.float32),
            pltpu.VMEM((8, width), jnp.float32),
            pltpu.SemaphoreType.DMA((row_tiles,)),
            pltpu.SemaphoreType.DMA((k_tiles,)),
        ],
        compiler_params=pltpu.CompilerParams(vmem_limit_bytes=VMEM_ALL),
        name="project",
    )(plan, prompt_spans, me, hidden, gain, w_kv, *tables)


def softmax_step(keys, values_t, q_ref, chunk, acc, row_max, masked=None):
    count = q_ref.shape[1] // chunk
    scores, weights, factors = {}, {}, {}
    for c in range(count + 2):
        if c < count:
            cols = slice(c * chunk, (c + 1) * chunk)
            scores[c] = jnp.dot(keys, q_ref[:, cols], preferred_element_type=jnp.float32)
        if c >= 2:
            cols = slice((c - 2) * chunk, (c - 1) * chunk)
            part = jnp.dot(values_t, weights.pop(c - 2), preferred_element_type=jnp.float32)
            acc[:, cols] = acc[:, cols] * factors.pop(c - 2) + part
        if 1 <= c <= count:
            cols = slice((c - 1) * chunk, c * chunk)
            s = scores.pop(c - 1)
            if masked is not None:
                s = masked(s)
            old = row_max[:, cols]
            new = jnp.maximum(old, jnp.max(s, axis=0, keepdims=True))
            factors[c - 1] = jnp.exp(old - new)
            row_max[:, cols] = new
            weights[c - 1] = jnp.exp(s - new).astype(jnp.bfloat16)


def queries_kernel(plan_ref, prompt_ref, me_ref, place_ref, q_ref, kv_ref, ci, si, co, so,
                   qt_ref, acc, row_max, sel_ref, vt):
    rows = q_ref.shape[0]
    head = ci.shape[1]
    heads = q_ref.shape[1] // head
    me = me_ref[0]
    own_span = plan_ref[me]
    _, depth = own_place(prompt_ref, own_span)
    cosine, sine = angles(depth, ci, si, co, so)
    for h in range(heads):
        x = q_ref[:, h * head:(h + 1) * head].astype(jnp.float32)
        x = (rotate(x, cosine, sine) * head ** (-0.5)).astype(jnp.bfloat16)
        qt_ref[:, h * rows:(h + 1) * rows] = x.T
    slots = sel_ref.shape[0]
    blocks = place_ref.shape[1]
    mine = (place_ref[0:1, :] == me) & (
        place_ref[1:2, :] == lax.broadcasted_iota(jnp.int32, (slots, blocks), 0))
    block_id = lax.broadcasted_iota(jnp.int32, (slots, blocks), 1).astype(jnp.float32)
    sel_ref[...] = jnp.sum(jnp.where(mine, block_id, 0.0), axis=1, keepdims=True).astype(jnp.int32)
    acc[...] = jnp.zeros_like(acc)
    row_max[...] = jnp.full_like(row_max, NEG)
    vt[head:, :] = jnp.ones((ONES, rows), jnp.bfloat16)
    vt[:head, :] = kv_ref[:, head:].T

    def causal(s):
        key = lax.broadcasted_iota(jnp.int32, s.shape, 0)
        row = lax.broadcasted_iota(jnp.int32, s.shape, 1)
        return jnp.where(key <= row, s, NEG)

    softmax_step(kv_ref[:, :head], vt[...], qt_ref, rows, acc, row_max, causal)


def prepare(plan, prompt_spans, me, place, queries, kv, tables):
    rows = queries.shape[0]
    head = kv.shape[1] // 2
    columns = rows * (queries.shape[1] // head)
    return pl.pallas_call(
        queries_kernel,
        out_shape=(
            jax.ShapeDtypeStruct((head, columns), jnp.bfloat16),
            jax.ShapeDtypeStruct((head + ONES, columns), jnp.float32),
            jax.ShapeDtypeStruct((1, columns), jnp.float32),
            jax.ShapeDtypeStruct((rows // BLK, 1), jnp.int32),
        ),
        in_specs=[SMEM_SPEC] * 3 + [VMEM_SPEC] * 7,
        out_specs=(VMEM_SPEC,) * 4,
        scratch_shapes=[pltpu.VMEM((head + ONES, rows), jnp.bfloat16)],
        compiler_params=pltpu.CompilerParams(vmem_limit_bytes=VMEM_PART),
        name="prepare",
    )(plan, prompt_spans, me, place, queries, kv, *tables)


def taken(known, done, most, even):
    count = jnp.minimum(known - done, most)
    return count // 2 * 2 if even else count


def attend_kernel(plan_ref, prompt_ref, me_ref, src_ref, *rest, before, blocks, old, cap, even, first_stage, last):
    sel_ref = None
    if last:
        sel_ref, *rest = rest
    qt_ref, acc_in, max_in, *rest = rest
    if not first_stage:
        rest = rest[1:]
    count = 1 + max(r for r, _ in blocks)
    refs, rest = rest[:count], rest[count:]
    if last:
        pool, ctx_ref, cache_ref, acc, row_max, kv, vt, sems, pool_sem, pairs, pair_sem = rest
    else:
        pool, acc, row_max, kv, vt, sems, pool_sem = rest
    head, columns = qt_ref.shape
    n = plan_ref.shape[0]
    rows = pool.shape[0] // n
    me = me_ref[0]
    own_span = plan_ref[me]
    first, _ = own_place(prompt_ref, own_span)
    spans, needed, rank = [], [], []
    seen = jnp.int32(0)
    for j in range(len(blocks)):
        span = plan_ref[src_ref[me * n + j]]
        take = (span >= first) & (span < own_span)
        spans.append(span)
        needed.append(take)
        rank.append(seen)
        seen = seen + take.astype(jnp.int32)
    rank.append(seen)
    done = jnp.int32(0)
    for arrived, most, pairs_only in before:
        done = done + taken(rank[arrived], done, most, pairs_only)
    todo = taken(seen, done, cap, even)

    def fetch(j, slot):
        operand, row = blocks[j]
        return pltpu.make_async_copy(
            refs[operand].at[pl.ds(row, rows)], kv.at[pl.ds(pl.multiple_of(slot * rows, rows), rows)], sems.at[slot])

    def keep(j):
        operand, row = blocks[j]
        return pltpu.make_async_copy(
            refs[operand].at[pl.ds(row, rows)],
            pool.at[pl.ds(pl.multiple_of(spans[j] * rows, rows), rows)], pool_sem)

    for j in range(len(blocks)):
        @pl.when(needed[j] & (rank[j] >= done) & (rank[j] < done + todo))
        def _():
            fetch(j, rank[j] - done).start()

    for j in range(old, len(blocks)):
        keep(j).start()
    acc[...] = acc_in[...]
    row_max[...] = max_in[...]
    vt[head:, :] = jnp.ones((ONES, vt.shape[1]), jnp.bfloat16)
    if last:
        tile = 2 * BLK
        for j in range(old, len(blocks)):
            keep(j).wait()

        def pair(slot):
            row = pl.multiple_of(sel_ref[slot, 0] // 2 * tile, tile)
            return pltpu.make_async_copy(
                pool.at[pl.ds(row, tile)], pairs.at[pl.ds(pl.multiple_of(slot * tile, tile), tile)], pair_sem)

        @pl.loop(0, cache_ref.shape[0])
        def _(slot):
            pair(slot).start()

    def visit(slot, many):
        for k in range(many):
            fetch(0, slot + k).wait()
        block = kv.at[pl.ds(pl.multiple_of(slot * rows, rows), many * rows)]
        vt[:head, :many * rows] = block[:, head:].T
        softmax_step(block[:, :head], vt[:, :many * rows], qt_ref, 512, acc, row_max)

    @pl.loop(0, todo // 2)
    def _(i):
        visit(2 * i, 2)

    if not even:
        @pl.when(todo % 2 == 1)
        def _():
            visit(todo - 1, 1)

    if not last:
        for j in range(old, len(blocks)):
            keep(j).wait()
        return
    for h in range(columns // rows):
        cols = slice(h * rows, (h + 1) * rows)
        out = acc[:head, cols] / acc[head:head + 1, cols]
        ctx_ref[:, h * head:(h + 1) * head] = out.astype(jnp.bfloat16).T

    @pl.loop(0, cache_ref.shape[0])
    def _(slot):
        pair(slot).wait()

    for slot in range(cache_ref.shape[0]):
        both = pairs[slot * tile:(slot + 1) * tile, :].astype(jnp.float32)
        odd = sel_ref[slot, 0] % 2 == 1
        cache_ref[slot] = jnp.where(odd, both[BLK:], both[:BLK]).astype(jnp.bfloat16)


def attend(plan, prompt_spans, me, sources, qt, state, arrays, blocks, old, before, cap, even, rows, sel=None):
    acc, row_max, *pool = state
    head, columns = qt.shape
    both = arrays[0].shape[1]
    last = sel is not None
    n = plan.shape[0]
    scratch = [
        pltpu.VMEM((cap * rows, both), jnp.bfloat16),
        pltpu.VMEM((head + ONES, 2 * rows), jnp.bfloat16),
        pltpu.SemaphoreType.DMA((cap,)),
        pltpu.SemaphoreType.DMA,
    ]
    carried = [jax.ShapeDtypeStruct(acc.shape, jnp.float32), jax.ShapeDtypeStruct(row_max.shape, jnp.float32)]
    out_shape = [jax.ShapeDtypeStruct((n * rows, both), jnp.bfloat16)]
    if last:
        out_shape += [
            jax.ShapeDtypeStruct((rows, columns // rows * head), jnp.bfloat16),
            jax.ShapeDtypeStruct((rows // BLK, BLK, both), jnp.bfloat16),
        ]
        scratch = [pltpu.VMEM(s.shape, s.dtype) for s in carried] + scratch
        scratch += [pltpu.VMEM((2 * rows, both), jnp.bfloat16), pltpu.SemaphoreType.DMA]
    else:
        out_shape += carried
    scalars = [plan, prompt_spans, me, sources] + ([sel] if last else [])
    work = 4 * head * columns * rows * min(cap, 4)
    aliases = {len(scalars) + 3: 0} if pool else {}
    return pl.pallas_call(
        functools.partial(attend_kernel, before=tuple(before), blocks=tuple(blocks), old=old, cap=cap, even=even,
                          first_stage=not pool, last=last),
        out_shape=tuple(out_shape),
        in_specs=[SMEM_SPEC] * len(scalars) + [VMEM_SPEC] * 3 + [ANY_SPEC] * (len(pool) + len(arrays)),
        out_specs=(ANY_SPEC,) + (VMEM_SPEC,) * 2,
        scratch_shapes=scratch,
        input_output_aliases=aliases,
        compiler_params=pltpu.CompilerParams(vmem_limit_bytes=VMEM_PART),
        cost_estimate=pl.CostEstimate(flops=2 * work, bytes_accessed=4 * 1024 * 1024, transcendentals=work // (4 * head)),
        name="finish" if last else "attend",
    )(*scalars, qt, acc, row_max, *pool, *arrays)


class Routes:
    def __init__(self, n):
        self.n = n
        self.lines = n // 8
        order = [0] + list(range(1, self.lines, 2)) + list(range(2, self.lines, 2))[::-1]
        following = {a: order[(i + 1) % self.lines] for i, a in enumerate(order)}
        preceding = {b: a for a, b in following.items()}
        self.ahead = [self.at(following[l], y, x, c) for l, y, x, c in self.all()]
        self.back = [self.at(preceding[l], y, x, c) for l, y, x, c in self.all()]
        self.flip_a = [self.at(l, y, 1 - x, c) if c == 0 else self.at(l, 1 - y, x, c) for l, y, x, c in self.all()]
        self.flip_b = [self.at(l, y, 1 - x, c) if c == 1 else self.at(l, 1 - y, x, c) for l, y, x, c in self.all()]
        self.core = [self.at(l, y, x, 1 - c) for l, y, x, c in self.all()]

    def all(self):
        return [(i // 8, (i // 4) % 2, (i // 2) % 2, i % 2) for i in range(self.n)]

    def at(self, line, y, x, core):
        return ((line * 2 + y) * 2 + x) * 2 + core


class Block:
    def __init__(self, array, sources):
        self.array, self.sources = array, sources

    def send(self, to):
        moved = []
        for source in self.sources:
            landed = [0] * len(to)
            for i, target in enumerate(to):
                landed[target] = source[i]
            moved.append(landed)
        return Block(lax.ppermute(self.array, "section", list(enumerate(to))), moved)


def join(parts):
    if len(parts) == 1:
        return parts[0]
    return Block(jnp.concatenate([p.array for p in parts], axis=0), [s for p in parts for s in p.sources])


CAPS = (4, 6, 4, 4)


def local(hidden, norm_gain, queries, w_kv, plan, prompt_spans, placement):
    n = lax.axis_size("section")
    rows = hidden.shape[0]
    head = w_kv.shape[1] // 2
    me = lax.axis_index("section").astype(jnp.int32).reshape(1)
    tables = rotary_tables(rows, head, n)
    kv = project(plan, prompt_spans, me, hidden, norm_gain, w_kv, tables)
    route = Routes(n)
    own = Block(kv, [list(range(n))])
    payload = ahead = back = own
    lines_left = route.lines - 1
    pending = []
    fresh = [own]
    arrived, before, old, phase = [own], [], 0, 0
    state = qt = sel = None

    def stage(cap, even, sel=None):
        arrays = [block.array for block in arrived]
        places = [(i, r * rows) for i, block in enumerate(arrived) for r in range(len(block.sources))]
        table = [source for block in arrived for source in block.sources]
        table = table + [[0] * n] * (n - len(table))
        sources = jnp.asarray(np.array(table, np.int32).T.reshape(-1))
        result = attend(plan, prompt_spans, me, sources, qt, state, arrays, places, old, before, cap, even, rows, sel)
        before.append((len(places), cap, even))
        return len(places), result

    while payload is not None or pending or fresh:
        crossed = [join(fresh).send(route.core)] if fresh else []
        passed = [p.send(route.flip_b) for p in pending]
        flipped, chain = [], []

        def flip():
            if payload is not None:
                b = payload.send(route.flip_b)
                flipped.extend([payload.send(route.flip_a), b])

        if phase > 0:
            ends = (lines_left > 0, lines_left > 1)
        else:
            flip()
            ends = (lines_left > 0, lines_left > 1)
        if ends[1]:
            back = back.send(route.back)
        if ends[0]:
            ahead = ahead.send(route.ahead)
        chain = ([ahead] if ends[0] else []) + ([back] if ends[1] else [])
        lines_left -= len(chain)
        if phase > 0:
            flip()
        if phase == 0:
            qt, acc, row_max, sel = prepare(plan, prompt_spans, me, placement.T, queries, kv, tables)
            state = (acc, row_max)
        else:
            old, (pool, acc, row_max) = stage(CAPS[min(phase - 1, len(CAPS) - 1)], phase > 1)
            state = (acc, row_max, pool)
        everything = chain + flipped + passed + crossed
        held, state = lax.optimization_barrier(([block.array for block in everything], state))
        for block, array in zip(everything, held):
            block.array = array
        payload = join(chain) if chain else None
        pending = flipped[:1]
        fresh = ([payload] if payload is not None else []) + flipped + passed
        arrived = arrived + crossed + fresh
        phase += 1
    _, (_, context, cache) = stage(n, False, sel)
    return context, cache


def solution(mesh):
    placed = (
        P(("cell", "section"), None),
        P(),
        P(("cell", "section"), None),
        P(),
        P("cell"),
        P("cell"),
        P("cell", None),
    )
    return jax.shard_map(
        local,
        mesh=mesh,
        in_specs=placed,
        out_specs=(P(("cell", "section"), None), P(("cell", "section"), None, None)),
        check_vma=False,
    )
```

```python
import functools

import jax
import jax.numpy as jnp
import numpy as np
from jax import lax
from jax.experimental import pallas as pl
from jax.experimental.pallas import tpu as pltpu
from jax.sharding import PartitionSpec as P

BLK = 8
THETA = 500000.0
EPS = 1e-05
ONES = 16
NEG = -1e30
VMEM_ALL = 56 * 1024 * 1024
VMEM_PART = 24 * 1024 * 1024
SMEM_SPEC = pl.BlockSpec(memory_space=pltpu.SMEM)
VMEM_SPEC = pl.BlockSpec(memory_space=pltpu.VMEM)
ANY_SPEC = pl.BlockSpec(memory_space=pl.ANY)


def rotary_tables(rows, head, spans):
    half = head // 2
    freq = THETA ** (-np.arange(half, dtype=np.float64) * 2.0 / head)
    freq = np.concatenate([freq, freq])
    inner = np.arange(rows, dtype=np.float64)[:, None] * freq
    outer = np.arange(spans, dtype=np.float64)[:, None] * rows * freq
    as32 = lambda a: jnp.asarray(a.astype(np.float32))
    return (as32(np.cos(inner)), as32(np.sin(inner)), as32(np.cos(outer)), as32(np.sin(outer)))


def own_place(prompt_ref, own_span):
    first = jnp.int32(0)
    end = jnp.int32(0)
    for p in range(prompt_ref.shape[0]):
        end = end + prompt_ref[p]
        first = jnp.where(own_span >= end, end, first)
    return first, own_span - first


def angles(depth, cos_in, sin_in, cos_out, sin_out):
    head = cos_in.shape[1]
    c0, s0 = cos_out[pl.ds(depth, 1), :], sin_out[pl.ds(depth, 1), :]
    c, s = cos_in[...], sin_in[...]
    cosine = c0 * c - s0 * s
    sine = s0 * c + c0 * s
    lane = lax.broadcasted_iota(jnp.int32, sine.shape, 1)
    return cosine, jnp.where(lane < head // 2, -sine, sine)


def rotate(x, cosine, sine):
    half = x.shape[1] // 2
    return x * cosine + jnp.concatenate([x[:, half:], x[:, :half]], axis=1) * sine


def project_kernel(plan_ref, prompt_ref, me_ref, hid_hbm, gain_ref, w_hbm, ci, si, co, so, kv_ref,
                   hid, w, scale, gain, hsem, wsem, *, group):
    rows, width = hid.shape
    head = kv_ref.shape[1] // 2
    row_tiles, k_tiles = hsem.shape[0], wsem.shape[0]
    rt, kt = rows // row_tiles, width // k_tiles
    lanes = scale.shape[1]
    hcopy = [pltpu.make_async_copy(hid_hbm.at[pl.ds(i * rt, rt)], hid.at[pl.ds(i * rt, rt)], hsem.at[i])
             for i in range(row_tiles)]
    wcopy = [pltpu.make_async_copy(w_hbm.at[pl.ds(i * kt, kt)], w.at[pl.ds(i * kt, kt)], wsem.at[i])
             for i in range(k_tiles)]
    for cp in hcopy + wcopy:
        cp.start()
    own_span = plan_ref[me_ref[0]]
    _, depth = own_place(prompt_ref, own_span)
    gain[...] = jnp.broadcast_to(gain_ref[...].astype(jnp.float32).reshape(1, width), gain.shape)

    def measure(row):
        sums = [jnp.zeros((group, lanes), jnp.float32)] * 4
        for j in range(width // lanes):
            x = hid[pl.ds(row, group), j * lanes:(j + 1) * lanes].astype(jnp.float32)
            sums[j % 4] = sums[j % 4] + x * x
        total = jnp.sum((sums[0] + sums[1]) + (sums[2] + sums[3]), axis=1, keepdims=True)
        scale[pl.ds(row, group), :] = jnp.broadcast_to(lax.rsqrt(total * (1.0 / width) + EPS), (group, lanes))

    def normalise(row):
        by = scale[pl.ds(row, group), :].reshape(group // 8, 8, lanes)
        for j in range(width // lanes):
            cols = slice(j * lanes, (j + 1) * lanes)
            x = hid[pl.ds(row, group), cols].astype(jnp.float32).reshape(group // 8, 8, lanes)
            hid[pl.ds(row, group), cols] = (x * by * gain[:, cols][None]).reshape(group, lanes).astype(jnp.bfloat16)

    for i in range(row_tiles + 1):
        if i < row_tiles:
            hcopy[i].wait()

        @pl.loop(0, rt // group)
        def _(g):
            if i < row_tiles:
                measure(pl.multiple_of(i * rt + g * group, group))
            if i > 0:
                normalise(pl.multiple_of((i - 1) * rt + g * group, group))

    cosine, sine = angles(depth, ci, si, co, so)
    for cp in wcopy:
        cp.wait()
    projected = jnp.dot(hid[...], w[...], preferred_element_type=jnp.float32)
    kv_ref[:, :head] = rotate(projected[:, :head], cosine, sine).astype(jnp.bfloat16)
    kv_ref[:, head:] = projected[:, head:].astype(jnp.bfloat16)


def project(plan, prompt_spans, me, hidden, gain, w_kv, tables):
    rows, width = hidden.shape
    row_tiles, k_tiles = 6, 4
    return pl.pallas_call(
        functools.partial(project_kernel, group=32),
        out_shape=jax.ShapeDtypeStruct((rows, w_kv.shape[1]), jnp.bfloat16),
        in_specs=[SMEM_SPEC] * 3 + [ANY_SPEC, VMEM_SPEC, ANY_SPEC] + [VMEM_SPEC] * 4,
        out_specs=VMEM_SPEC,
        scratch_shapes=[
            pltpu.VMEM((rows, width), jnp.bfloat16),
            pltpu.VMEM(w_kv.shape, jnp.bfloat16),
            pltpu.VMEM((rows, 128), jnp.float32),
            pltpu.VMEM((8, width), jnp.float32),
            pltpu.SemaphoreType.DMA((row_tiles,)),
            pltpu.SemaphoreType.DMA((k_tiles,)),
        ],
        compiler_params=pltpu.CompilerParams(vmem_limit_bytes=VMEM_ALL),
        name="project",
    )(plan, prompt_spans, me, hidden, gain, w_kv, *tables)


def softmax_step(keys, values_t, q_ref, chunk, acc, row_max, masked=None):
    count = q_ref.shape[1] // chunk
    scores, weights, factors = {}, {}, {}
    for c in range(count + 2):
        if c < count:
            cols = slice(c * chunk, (c + 1) * chunk)
            scores[c] = jnp.dot(keys, q_ref[:, cols], preferred_element_type=jnp.float32)
        if c >= 2:
            cols = slice((c - 2) * chunk, (c - 1) * chunk)
            part = jnp.dot(values_t, weights.pop(c - 2), preferred_element_type=jnp.float32)
            acc[:, cols] = acc[:, cols] * factors.pop(c - 2) + part
        if 1 <= c <= count:
            cols = slice((c - 1) * chunk, c * chunk)
            s = scores.pop(c - 1)
            if masked is not None:
                s = masked(s)
            old = row_max[:, cols]
            new = jnp.maximum(old, jnp.max(s, axis=0, keepdims=True))
            factors[c - 1] = jnp.exp(old - new)
            row_max[:, cols] = new
            weights[c - 1] = jnp.exp(s - new).astype(jnp.bfloat16)


def queries_kernel(plan_ref, prompt_ref, me_ref, place_ref, q_ref, kv_ref, ci, si, co, so,
                   qt_ref, acc, row_max, sel_ref, vt):
    rows = q_ref.shape[0]
    head = ci.shape[1]
    heads = q_ref.shape[1] // head
    me = me_ref[0]
    own_span = plan_ref[me]
    _, depth = own_place(prompt_ref, own_span)
    cosine, sine = angles(depth, ci, si, co, so)
    for h in range(heads):
        x = q_ref[:, h * head:(h + 1) * head].astype(jnp.float32)
        x = (rotate(x, cosine, sine) * head ** (-0.5)).astype(jnp.bfloat16)
        qt_ref[:, h * rows:(h + 1) * rows] = x.T
    slots = sel_ref.shape[0]
    blocks = place_ref.shape[1]
    mine = (place_ref[0:1, :] == me) & (
        place_ref[1:2, :] == lax.broadcasted_iota(jnp.int32, (slots, blocks), 0))
    block_id = lax.broadcasted_iota(jnp.int32, (slots, blocks), 1).astype(jnp.float32)
    sel_ref[...] = jnp.sum(jnp.where(mine, block_id, 0.0), axis=1, keepdims=True).astype(jnp.int32)
    acc[...] = jnp.zeros_like(acc)
    row_max[...] = jnp.full_like(row_max, NEG)
    vt[head:, :] = jnp.ones((ONES, rows), jnp.bfloat16)
    vt[:head, :] = kv_ref[:, head:].T

    def causal(s):
        key = lax.broadcasted_iota(jnp.int32, s.shape, 0)
        row = lax.broadcasted_iota(jnp.int32, s.shape, 1)
        return jnp.where(key <= row, s, NEG)

    softmax_step(kv_ref[:, :head], vt[...], qt_ref, rows, acc, row_max, causal)


def prepare(plan, prompt_spans, me, place, queries, kv, tables):
    rows = queries.shape[0]
    head = kv.shape[1] // 2
    columns = rows * (queries.shape[1] // head)
    return pl.pallas_call(
        queries_kernel,
        out_shape=(
            jax.ShapeDtypeStruct((head, columns), jnp.bfloat16),
            jax.ShapeDtypeStruct((head + ONES, columns), jnp.float32),
            jax.ShapeDtypeStruct((1, columns), jnp.float32),
            jax.ShapeDtypeStruct((rows // BLK, 1), jnp.int32),
        ),
        in_specs=[SMEM_SPEC] * 3 + [VMEM_SPEC] * 7,
        out_specs=(VMEM_SPEC,) * 4,
        scratch_shapes=[pltpu.VMEM((head + ONES, rows), jnp.bfloat16)],
        compiler_params=pltpu.CompilerParams(vmem_limit_bytes=VMEM_PART),
        name="prepare",
    )(plan, prompt_spans, me, place, queries, kv, *tables)


def taken(known, done, most, even):
    count = jnp.minimum(known - done, most)
    return count // 2 * 2 if even else count


def attend_kernel(plan_ref, prompt_ref, me_ref, src_ref, *rest, before, blocks, cap, even, last):
    sel_ref = None
    if last:
        sel_ref, *rest = rest
    qt_ref, acc_in, max_in, *rest = rest
    count = 1 + max(r for r, _ in blocks)
    refs, rest = rest[:count], rest[count:]
    if last:
        ctx_ref, cache_ref, acc, row_max, kv, vt, goes = rest
    else:
        acc, row_max, kv, vt = rest
    head, columns = qt_ref.shape
    n = plan_ref.shape[0]
    rows = kv.shape[0] // cap
    me = me_ref[0]
    own_span = plan_ref[me]
    first, _ = own_place(prompt_ref, own_span)
    spans, needed, rank = [], [], []
    seen = jnp.int32(0)
    for j in range(len(blocks)):
        span = plan_ref[src_ref[me * n + j]]
        take = (span >= first) & (span < own_span)
        spans.append(span)
        needed.append(take)
        rank.append(seen)
        seen = seen + take.astype(jnp.int32)
    rank.append(seen)
    done = jnp.int32(0)
    for arrived, most, pairs_only in before:
        done = done + taken(rank[arrived], done, most, pairs_only)
    todo = taken(seen, done, cap, even)
    for j, (operand, row) in enumerate(blocks):
        slot = rank[j] - done

        @pl.when(needed[j] & (slot >= 0) & (slot < todo))
        def _():
            kv[pl.ds(pl.multiple_of(slot * rows, rows), rows), :] = refs[operand][row:row + rows, :]

    acc[...] = acc_in[...]
    row_max[...] = max_in[...]
    vt[head:, :] = jnp.ones((ONES, vt.shape[1]), jnp.bfloat16)

    def visit(slot, many):
        block = kv.at[pl.ds(pl.multiple_of(slot * rows, rows), many * rows)]
        vt[:head, :many * rows] = block[:, head:].T
        softmax_step(block[:, :head], vt[:, :many * rows], qt_ref, 512, acc, row_max)

    @pl.loop(0, todo // 2)
    def _(i):
        visit(2 * i, 2)

    if not even:
        @pl.when(todo % 2 == 1)
        def _():
            visit(todo - 1, 1)

    if not last:
        return
    for h in range(columns // rows):
        cols = slice(h * rows, (h + 1) * rows)
        out = acc[:head, cols] / acc[head:head + 1, cols]
        ctx_ref[:, h * head:(h + 1) * head] = out.astype(jnp.bfloat16).T

    per_span = rows // BLK

    @pl.loop(0, 2 * n)
    def _(i):
        goes[i] = jnp.int32(-1)

    @pl.loop(0, cache_ref.shape[0])
    def _(slot):
        at = 2 * (sel_ref[slot, 0] // per_span)
        goes[jnp.where(goes[at] < 0, at, at + 1)] = slot

    for j, (operand, row) in enumerate(blocks):
        @pl.when(goes[2 * spans[j]] >= 0)
        def _():
            for k in range(2):
                slot = goes[2 * spans[j] + k]
                block = sel_ref[slot, 0] - spans[j] * per_span
                start = pl.multiple_of(block // 2 * (2 * BLK), 2 * BLK)
                pair = refs[operand][pl.ds(row + start, 2 * BLK), :].astype(jnp.float32)
                cache_ref[slot] = jnp.where(block % 2 == 1, pair[BLK:], pair[:BLK]).astype(jnp.bfloat16)


def attend(plan, prompt_spans, me, sources, qt, state, arrays, blocks, before, cap, even, rows, sel=None):
    acc, row_max = state
    head, columns = qt.shape
    both = arrays[0].shape[1]
    last = sel is not None
    n = plan.shape[0]
    scratch = [
        pltpu.VMEM((cap * rows, both), jnp.bfloat16),
        pltpu.VMEM((head + ONES, 2 * rows), jnp.bfloat16),
    ]
    carried = [jax.ShapeDtypeStruct(acc.shape, jnp.float32), jax.ShapeDtypeStruct(row_max.shape, jnp.float32)]
    out_shape = carried
    if last:
        out_shape = [
            jax.ShapeDtypeStruct((rows, columns // rows * head), jnp.bfloat16),
            jax.ShapeDtypeStruct((rows // BLK, BLK, both), jnp.bfloat16),
        ]
        scratch = [pltpu.VMEM(s.shape, s.dtype) for s in carried] + scratch + [pltpu.SMEM((2 * n,), jnp.int32)]
    scalars = [plan, prompt_spans, me, sources] + ([sel] if last else [])
    work = 4 * head * columns * rows * min(cap, 4)
    return pl.pallas_call(
        functools.partial(attend_kernel, before=tuple(before), blocks=tuple(blocks), cap=cap, even=even, last=last),
        out_shape=tuple(out_shape),
        in_specs=[SMEM_SPEC] * len(scalars) + [VMEM_SPEC] * (3 + len(arrays)),
        out_specs=(VMEM_SPEC,) * 2,
        scratch_shapes=scratch,
        compiler_params=pltpu.CompilerParams(vmem_limit_bytes=VMEM_PART),
        cost_estimate=pl.CostEstimate(flops=2 * work, bytes_accessed=4 * 1024 * 1024, transcendentals=work // (4 * head)),
        name="finish" if last else "attend",
    )(*scalars, qt, acc, row_max, *arrays)


class Routes:
    def __init__(self, n):
        self.n = n
        self.lines = n // 8
        order = [0] + list(range(1, self.lines, 2)) + list(range(2, self.lines, 2))[::-1]
        following = {a: order[(i + 1) % self.lines] for i, a in enumerate(order)}
        preceding = {b: a for a, b in following.items()}
        self.ahead = [self.at(following[l], y, x, c) for l, y, x, c in self.all()]
        self.back = [self.at(preceding[l], y, x, c) for l, y, x, c in self.all()]
        self.flip_a = [self.at(l, y, 1 - x, c) if c == 0 else self.at(l, 1 - y, x, c) for l, y, x, c in self.all()]
        self.flip_b = [self.at(l, y, 1 - x, c) if c == 1 else self.at(l, 1 - y, x, c) for l, y, x, c in self.all()]
        self.core = [self.at(l, y, x, 1 - c) for l, y, x, c in self.all()]

    def all(self):
        return [(i // 8, (i // 4) % 2, (i // 2) % 2, i % 2) for i in range(self.n)]

    def at(self, line, y, x, core):
        return ((line * 2 + y) * 2 + x) * 2 + core


class Block:
    def __init__(self, array, sources):
        self.array, self.sources = array, sources

    def send(self, to):
        moved = []
        for source in self.sources:
            landed = [0] * len(to)
            for i, target in enumerate(to):
                landed[target] = source[i]
            moved.append(landed)
        return Block(lax.ppermute(self.array, "section", list(enumerate(to))), moved)


def join(parts):
    if len(parts) == 1:
        return parts[0]
    return Block(jnp.concatenate([p.array for p in parts], axis=0), [s for p in parts for s in p.sources])


CAPS = (4, 6, 4, 4)


def local(hidden, norm_gain, queries, w_kv, plan, prompt_spans, placement):
    n = lax.axis_size("section")
    rows = hidden.shape[0]
    head = w_kv.shape[1] // 2
    me = lax.axis_index("section").astype(jnp.int32).reshape(1)
    tables = rotary_tables(rows, head, n)
    kv = project(plan, prompt_spans, me, hidden, norm_gain, w_kv, tables)
    route = Routes(n)
    own = Block(kv, [list(range(n))])
    payload = ahead = back = own
    lines_left = route.lines - 1
    pending = []
    fresh = [own]
    arrived, before, phase = [own], [], 0
    state = qt = sel = None

    def stage(cap, even, sel=None):
        arrays = [block.array for block in arrived]
        places = [(i, r * rows) for i, block in enumerate(arrived) for r in range(len(block.sources))]
        table = [source for block in arrived for source in block.sources]
        table = table + [[0] * n] * (n - len(table))
        sources = jnp.asarray(np.array(table, np.int32).T.reshape(-1))
        result = attend(plan, prompt_spans, me, sources, qt, state, arrays, places, before, cap, even, rows, sel)
        before.append((len(places), cap, even))
        return result

    while payload is not None or pending or fresh:
        crossed = [join(fresh).send(route.core)] if fresh else []
        passed = [p.send(route.flip_b) for p in pending]
        flipped, chain = [], []

        def flip():
            if payload is not None:
                b = payload.send(route.flip_b)
                flipped.extend([payload.send(route.flip_a), b])

        if phase > 0:
            ends = (lines_left > 0, lines_left > 1)
        else:
            flip()
            ends = (lines_left > 0, lines_left > 1)
        if ends[1]:
            back = back.send(route.back)
        if ends[0]:
            ahead = ahead.send(route.ahead)
        chain = ([ahead] if ends[0] else []) + ([back] if ends[1] else [])
        lines_left -= len(chain)
        if phase > 0:
            flip()
        if phase == 0:
            qt, acc, row_max, sel = prepare(plan, prompt_spans, me, placement.T, queries, kv, tables)
            state = (acc, row_max)
        else:
            state = stage(CAPS[min(phase - 1, len(CAPS) - 1)], phase > 1)
        everything = chain + flipped + passed + crossed
        held, state = lax.optimization_barrier(([block.array for block in everything], state))
        for block, array in zip(everything, held):
            block.array = array
        payload = join(chain) if chain else None
        pending = flipped[:1]
        fresh = ([payload] if payload is not None else []) + flipped + passed
        arrived = arrived + crossed + fresh
        phase += 1
    return stage(n, False, sel)


def solution(mesh):
    placed = (
        P(("cell", "section"), None),
        P(),
        P(("cell", "section"), None),
        P(),
        P("cell"),
        P("cell"),
        P("cell", None),
    )
    return jax.shard_map(
        local,
        mesh=mesh,
        in_specs=placed,
        out_specs=(P(("cell", "section"), None), P(("cell", "section"), None, None)),
        check_vma=False,
    )
```

```python
import functools

import jax
import jax.numpy as jnp
import numpy as np
from jax import lax
from jax.experimental import pallas as pl
from jax.experimental.pallas import tpu as pltpu
from jax.sharding import PartitionSpec as P

BLK = 8
THETA = 500000.0
EPS = 1e-05
ONES = 16
NEG = -1e30
VMEM_ALL = 56 * 1024 * 1024
VMEM_PART = 24 * 1024 * 1024
SMEM_SPEC = pl.BlockSpec(memory_space=pltpu.SMEM)
VMEM_SPEC = pl.BlockSpec(memory_space=pltpu.VMEM)
ANY_SPEC = pl.BlockSpec(memory_space=pl.ANY)


def rotary_tables(rows, head, spans):
    half = head // 2
    freq = THETA ** (-np.arange(half, dtype=np.float64) * 2.0 / head)
    freq = np.concatenate([freq, freq])
    inner = np.arange(rows, dtype=np.float64)[:, None] * freq
    outer = np.arange(spans, dtype=np.float64)[:, None] * rows * freq
    as32 = lambda a: jnp.asarray(a.astype(np.float32))
    return (as32(np.cos(inner)), as32(np.sin(inner)), as32(np.cos(outer)), as32(np.sin(outer)))


def own_place(prompt_ref, own_span):
    first = jnp.int32(0)
    end = jnp.int32(0)
    for p in range(prompt_ref.shape[0]):
        end = end + prompt_ref[p]
        first = jnp.where(own_span >= end, end, first)
    return first, own_span - first


def angles(depth, cos_in, sin_in, cos_out, sin_out):
    head = cos_in.shape[1]
    c0, s0 = cos_out[pl.ds(depth, 1), :], sin_out[pl.ds(depth, 1), :]
    c, s = cos_in[...], sin_in[...]
    cosine = c0 * c - s0 * s
    sine = s0 * c + c0 * s
    lane = lax.broadcasted_iota(jnp.int32, sine.shape, 1)
    return cosine, jnp.where(lane < head // 2, -sine, sine)


def rotate(x, cosine, sine):
    half = x.shape[1] // 2
    return x * cosine + jnp.concatenate([x[:, half:], x[:, :half]], axis=1) * sine


def project_kernel(plan_ref, prompt_ref, me_ref, hid_hbm, gain_ref, w_hbm, ci, si, co, so, kv_ref,
                   hid, w, scale, gain, hsem, wsem, *, group):
    rows, width = hid.shape
    head = kv_ref.shape[1] // 2
    row_tiles, k_tiles = hsem.shape[0], wsem.shape[0]
    rt, kt = rows // row_tiles, width // k_tiles
    lanes = scale.shape[1]
    hcopy = [pltpu.make_async_copy(hid_hbm.at[pl.ds(i * rt, rt)], hid.at[pl.ds(i * rt, rt)], hsem.at[i])
             for i in range(row_tiles)]
    wcopy = [pltpu.make_async_copy(w_hbm.at[pl.ds(i * kt, kt)], w.at[pl.ds(i * kt, kt)], wsem.at[i])
             for i in range(k_tiles)]
    for cp in hcopy + wcopy:
        cp.start()
    own_span = plan_ref[me_ref[0]]
    _, depth = own_place(prompt_ref, own_span)
    gain[...] = jnp.broadcast_to(gain_ref[...].astype(jnp.float32).reshape(1, width), gain.shape)

    def measure(row):
        sums = [jnp.zeros((group, lanes), jnp.float32)] * 4
        for j in range(width // lanes):
            x = hid[pl.ds(row, group), j * lanes:(j + 1) * lanes].astype(jnp.float32)
            sums[j % 4] = sums[j % 4] + x * x
        total = jnp.sum((sums[0] + sums[1]) + (sums[2] + sums[3]), axis=1, keepdims=True)
        scale[pl.ds(row, group), :] = jnp.broadcast_to(lax.rsqrt(total * (1.0 / width) + EPS), (group, lanes))

    def normalise(row):
        by = scale[pl.ds(row, group), :].reshape(group // 8, 8, lanes)
        for j in range(width // lanes):
            cols = slice(j * lanes, (j + 1) * lanes)
            x = hid[pl.ds(row, group), cols].astype(jnp.float32).reshape(group // 8, 8, lanes)
            hid[pl.ds(row, group), cols] = (x * by * gain[:, cols][None]).reshape(group, lanes).astype(jnp.bfloat16)

    for i in range(row_tiles + 1):
        if i < row_tiles:
            hcopy[i].wait()

        @pl.loop(0, rt // group)
        def _(g):
            if i < row_tiles:
                measure(pl.multiple_of(i * rt + g * group, group))
            if i > 0:
                normalise(pl.multiple_of((i - 1) * rt + g * group, group))

    cosine, sine = angles(depth, ci, si, co, so)
    for cp in wcopy:
        cp.wait()
    projected = jnp.dot(hid[...], w[...], preferred_element_type=jnp.float32)
    kv_ref[:, :head] = rotate(projected[:, :head], cosine, sine).astype(jnp.bfloat16)
    kv_ref[:, head:] = projected[:, head:].astype(jnp.bfloat16)


def project(plan, prompt_spans, me, hidden, gain, w_kv, tables):
    rows, width = hidden.shape
    row_tiles, k_tiles = 12, 4
    return pl.pallas_call(
        functools.partial(project_kernel, group=32),
        out_shape=jax.ShapeDtypeStruct((rows, w_kv.shape[1]), jnp.bfloat16),
        in_specs=[SMEM_SPEC] * 3 + [ANY_SPEC, VMEM_SPEC, ANY_SPEC] + [VMEM_SPEC] * 4,
        out_specs=VMEM_SPEC,
        scratch_shapes=[
            pltpu.VMEM((rows, width), jnp.bfloat16),
            pltpu.VMEM(w_kv.shape, jnp.bfloat16),
            pltpu.VMEM((rows, 128), jnp.float32),
            pltpu.VMEM((8, width), jnp.float32),
            pltpu.SemaphoreType.DMA((row_tiles,)),
            pltpu.SemaphoreType.DMA((k_tiles,)),
        ],
        compiler_params=pltpu.CompilerParams(vmem_limit_bytes=VMEM_ALL),
        name="project",
    )(plan, prompt_spans, me, hidden, gain, w_kv, *tables)


def softmax_step(keys, values_t, q_ref, chunk, acc, row_max, masked=None):
    count = q_ref.shape[1] // chunk
    scores, weights, factors = {}, {}, {}
    for c in range(count + 2):
        if c < count:
            cols = slice(c * chunk, (c + 1) * chunk)
            scores[c] = jnp.dot(keys, q_ref[:, cols], preferred_element_type=jnp.float32)
        if c >= 2:
            cols = slice((c - 2) * chunk, (c - 1) * chunk)
            part = jnp.dot(values_t, weights.pop(c - 2), preferred_element_type=jnp.float32)
            acc[:, cols] = acc[:, cols] * factors.pop(c - 2) + part
        if 1 <= c <= count:
            cols = slice((c - 1) * chunk, c * chunk)
            s = scores.pop(c - 1)
            if masked is not None:
                s = masked(s)
            old = row_max[:, cols]
            new = jnp.maximum(old, jnp.max(s, axis=0, keepdims=True))
            factors[c - 1] = jnp.exp(old - new)
            row_max[:, cols] = new
            weights[c - 1] = jnp.exp(s - new).astype(jnp.bfloat16)


def queries_kernel(plan_ref, prompt_ref, me_ref, place_ref, q_ref, kv_ref, ci, si, co, so,
                   qt_ref, acc, row_max, sel_ref, vt):
    rows = q_ref.shape[0]
    head = ci.shape[1]
    heads = q_ref.shape[1] // head
    me = me_ref[0]
    own_span = plan_ref[me]
    _, depth = own_place(prompt_ref, own_span)
    cosine, sine = angles(depth, ci, si, co, so)
    for h in range(heads):
        x = q_ref[:, h * head:(h + 1) * head].astype(jnp.float32)
        x = (rotate(x, cosine, sine) * head ** (-0.5)).astype(jnp.bfloat16)
        qt_ref[:, h * rows:(h + 1) * rows] = x.T
    slots = sel_ref.shape[0]
    blocks = place_ref.shape[1]
    mine = (place_ref[0:1, :] == me) & (
        place_ref[1:2, :] == lax.broadcasted_iota(jnp.int32, (slots, blocks), 0))
    block_id = lax.broadcasted_iota(jnp.int32, (slots, blocks), 1).astype(jnp.float32)
    sel_ref[...] = jnp.sum(jnp.where(mine, block_id, 0.0), axis=1, keepdims=True).astype(jnp.int32)
    acc[...] = jnp.zeros_like(acc)
    row_max[...] = jnp.full_like(row_max, NEG)
    vt[head:, :] = jnp.ones((ONES, rows), jnp.bfloat16)
    vt[:head, :] = kv_ref[:, head:].T

    def causal(s):
        key = lax.broadcasted_iota(jnp.int32, s.shape, 0)
        row = lax.broadcasted_iota(jnp.int32, s.shape, 1)
        return jnp.where(key <= row, s, NEG)

    softmax_step(kv_ref[:, :head], vt[...], qt_ref, rows, acc, row_max, causal)


def prepare(plan, prompt_spans, me, place, queries, kv, tables):
    rows = queries.shape[0]
    head = kv.shape[1] // 2
    columns = rows * (queries.shape[1] // head)
    return pl.pallas_call(
        queries_kernel,
        out_shape=(
            jax.ShapeDtypeStruct((head, columns), jnp.bfloat16),
            jax.ShapeDtypeStruct((head + ONES, columns), jnp.float32),
            jax.ShapeDtypeStruct((1, columns), jnp.float32),
            jax.ShapeDtypeStruct((rows // BLK, 1), jnp.int32),
        ),
        in_specs=[SMEM_SPEC] * 3 + [VMEM_SPEC] * 7,
        out_specs=(VMEM_SPEC,) * 4,
        scratch_shapes=[pltpu.VMEM((head + ONES, rows), jnp.bfloat16)],
        compiler_params=pltpu.CompilerParams(vmem_limit_bytes=VMEM_PART),
        name="prepare",
    )(plan, prompt_spans, me, place, queries, kv, *tables)


def taken(known, done, most, even):
    count = jnp.minimum(known - done, most)
    return count // 2 * 2 if even else count


def attend_kernel(plan_ref, prompt_ref, me_ref, src_ref, *rest, before, blocks, cap, even, last):
    sel_ref = None
    if last:
        sel_ref, *rest = rest
    qt_ref, acc_in, max_in, *rest = rest
    count = 1 + max(r for r, _ in blocks)
    refs, rest = rest[:count], rest[count:]
    if last:
        ctx_ref, cache_ref, acc, row_max, kv, vt, goes = rest
    else:
        acc, row_max, kv, vt = rest
    head, columns = qt_ref.shape
    n = plan_ref.shape[0]
    rows = kv.shape[0] // cap
    me = me_ref[0]
    own_span = plan_ref[me]
    first, _ = own_place(prompt_ref, own_span)
    spans, needed, rank = [], [], []
    seen = jnp.int32(0)
    for j in range(len(blocks)):
        span = plan_ref[src_ref[me * n + j]]
        take = (span >= first) & (span < own_span)
        spans.append(span)
        needed.append(take)
        rank.append(seen)
        seen = seen + take.astype(jnp.int32)
    rank.append(seen)
    done = jnp.int32(0)
    for arrived, most, pairs_only in before:
        done = done + taken(rank[arrived], done, most, pairs_only)
    todo = taken(seen, done, cap, even)
    for j, (operand, row) in enumerate(blocks):
        slot = rank[j] - done

        @pl.when(needed[j] & (slot >= 0) & (slot < todo))
        def _():
            kv[pl.ds(pl.multiple_of(slot * rows, rows), rows), :] = refs[operand][row:row + rows, :]

    acc[...] = acc_in[...]
    row_max[...] = max_in[...]
    vt[head:, :] = jnp.ones((ONES, vt.shape[1]), jnp.bfloat16)

    def visit(slot, many):
        block = kv.at[pl.ds(pl.multiple_of(slot * rows, rows), many * rows)]
        vt[:head, :many * rows] = block[:, head:].T
        softmax_step(block[:, :head], vt[:, :many * rows], qt_ref, 512, acc, row_max)

    @pl.loop(0, todo // 2)
    def _(i):
        visit(2 * i, 2)

    if not even:
        @pl.when(todo % 2 == 1)
        def _():
            visit(todo - 1, 1)

    if not last:
        return
    for h in range(columns // rows):
        cols = slice(h * rows, (h + 1) * rows)
        out = acc[:head, cols] * (1.0 / acc[head:head + 1, cols])
        ctx_ref[:, h * head:(h + 1) * head] = out.astype(jnp.bfloat16).T

    per_span = rows // BLK

    for i in range(2 * n):
        goes[i] = jnp.int32(-1)

    @pl.loop(0, cache_ref.shape[0], unroll=4)
    def _(slot):
        at = 2 * (sel_ref[slot, 0] // per_span)
        goes[jnp.where(goes[at] < 0, at, at + 1)] = slot

    for j, (operand, row) in enumerate(blocks):
        @pl.when(goes[2 * spans[j]] >= 0)
        def _():
            for k in range(2):
                slot = goes[2 * spans[j] + k]
                block = sel_ref[slot, 0] - spans[j] * per_span
                start = pl.multiple_of(block // 2 * (2 * BLK), 2 * BLK)
                pair = refs[operand][pl.ds(row + start, 2 * BLK), :].astype(jnp.float32)
                cache_ref[slot] = jnp.where(block % 2 == 1, pair[BLK:], pair[:BLK]).astype(jnp.bfloat16)


def attend(plan, prompt_spans, me, sources, qt, state, arrays, blocks, before, cap, even, rows, sel=None):
    acc, row_max = state
    head, columns = qt.shape
    both = arrays[0].shape[1]
    last = sel is not None
    n = plan.shape[0]
    scratch = [
        pltpu.VMEM((cap * rows, both), jnp.bfloat16),
        pltpu.VMEM((head + ONES, 2 * rows), jnp.bfloat16),
    ]
    carried = [jax.ShapeDtypeStruct(acc.shape, jnp.float32), jax.ShapeDtypeStruct(row_max.shape, jnp.float32)]
    out_shape = carried
    if last:
        out_shape = [
            jax.ShapeDtypeStruct((rows, columns // rows * head), jnp.bfloat16),
            jax.ShapeDtypeStruct((rows // BLK, BLK, both), jnp.bfloat16),
        ]
        scratch = [pltpu.VMEM(s.shape, s.dtype) for s in carried] + scratch + [pltpu.SMEM((2 * n,), jnp.int32)]
    scalars = [plan, prompt_spans, me, sources] + ([sel] if last else [])
    work = 4 * head * columns * rows * min(cap, 4)
    return pl.pallas_call(
        functools.partial(attend_kernel, before=tuple(before), blocks=tuple(blocks), cap=cap, even=even, last=last),
        out_shape=tuple(out_shape),
        in_specs=[SMEM_SPEC] * len(scalars) + [VMEM_SPEC] * (3 + len(arrays)),
        out_specs=(VMEM_SPEC,) * 2,
        scratch_shapes=scratch,
        compiler_params=pltpu.CompilerParams(vmem_limit_bytes=VMEM_PART),
        cost_estimate=pl.CostEstimate(flops=2 * work, bytes_accessed=4 * 1024 * 1024, transcendentals=work // (4 * head)),
        name="finish" if last else "attend",
    )(*scalars, qt, acc, row_max, *arrays)


class Routes:
    def __init__(self, n):
        self.n = n
        self.lines = n // 8
        order = [0] + list(range(1, self.lines, 2)) + list(range(2, self.lines, 2))[::-1]
        following = {a: order[(i + 1) % self.lines] for i, a in enumerate(order)}
        preceding = {b: a for a, b in following.items()}
        self.ahead = [self.at(following[l], y, x, c) for l, y, x, c in self.all()]
        self.back = [self.at(preceding[l], y, x, c) for l, y, x, c in self.all()]
        self.flip_a = [self.at(l, y, 1 - x, c) if c == 0 else self.at(l, 1 - y, x, c) for l, y, x, c in self.all()]
        self.flip_b = [self.at(l, y, 1 - x, c) if c == 1 else self.at(l, 1 - y, x, c) for l, y, x, c in self.all()]
        self.core = [self.at(l, y, x, 1 - c) for l, y, x, c in self.all()]

    def all(self):
        return [(i // 8, (i // 4) % 2, (i // 2) % 2, i % 2) for i in range(self.n)]

    def at(self, line, y, x, core):
        return ((line * 2 + y) * 2 + x) * 2 + core


class Block:
    def __init__(self, array, sources):
        self.array, self.sources = array, sources

    def send(self, to):
        moved = []
        for source in self.sources:
            landed = [0] * len(to)
            for i, target in enumerate(to):
                landed[target] = source[i]
            moved.append(landed)
        return Block(lax.ppermute(self.array, "section", list(enumerate(to))), moved)


def join(parts):
    if len(parts) == 1:
        return parts[0]
    return Block(jnp.concatenate([p.array for p in parts], axis=0), [s for p in parts for s in p.sources])


CAPS = (4, 6, 4, 4)


def local(hidden, norm_gain, queries, w_kv, plan, prompt_spans, placement):
    n = lax.axis_size("section")
    rows = hidden.shape[0]
    head = w_kv.shape[1] // 2
    me = lax.axis_index("section").astype(jnp.int32).reshape(1)
    tables = rotary_tables(rows, head, n)
    kv = project(plan, prompt_spans, me, hidden, norm_gain, w_kv, tables)
    route = Routes(n)
    own = Block(kv, [list(range(n))])
    payload = ahead = back = own
    lines_left = route.lines - 1
    pending = []
    fresh = [own]
    arrived, before, phase = [own], [], 0
    state = qt = sel = None

    def stage(cap, even, sel=None):
        arrays = [block.array for block in arrived]
        places = [(i, r * rows) for i, block in enumerate(arrived) for r in range(len(block.sources))]
        table = [source for block in arrived for source in block.sources]
        table = table + [[0] * n] * (n - len(table))
        sources = jnp.asarray(np.array(table, np.int32).T.reshape(-1))
        result = attend(plan, prompt_spans, me, sources, qt, state, arrays, places, before, cap, even, rows, sel)
        before.append((len(places), cap, even))
        return result

    while payload is not None or pending or fresh:
        crossed = [join(fresh).send(route.core)] if fresh else []
        passed = [p.send(route.flip_b) for p in pending]
        flipped, chain = [], []

        def flip():
            if payload is not None:
                b = payload.send(route.flip_b)
                flipped.extend([payload.send(route.flip_a), b])

        if phase > 0:
            ends = (lines_left > 0, lines_left > 1)
        else:
            flip()
            ends = (lines_left > 0, lines_left > 1)
        if ends[1]:
            back = back.send(route.back)
        if ends[0]:
            ahead = ahead.send(route.ahead)
        chain = ([ahead] if ends[0] else []) + ([back] if ends[1] else [])
        lines_left -= len(chain)
        if phase > 0:
            flip()
        if phase == 0:
            qt, acc, row_max, sel = prepare(plan, prompt_spans, me, placement.T, queries, kv, tables)
            state = (acc, row_max)
        else:
            state = stage(CAPS[min(phase - 1, len(CAPS) - 1)], phase > 1)
        everything = crossed + passed + (flipped + chain if phase == 0 else chain + flipped)
        held, state = lax.optimization_barrier(([block.array for block in everything], state))
        for block, array in zip(everything, held):
            block.array = array
        payload = join(chain) if chain else None
        pending = flipped[:1]
        if len(chain) > 1:
            waiting = [payload] + chain + pending
            held = lax.optimization_barrier([block.array for block in waiting])
            for block, array in zip(waiting, held):
                block.array = array
        fresh = ([payload] if payload is not None else []) + flipped + passed
        arrived = arrived + crossed + fresh
        phase += 1
    return stage(n, False, sel)


def solution(mesh):
    placed = (
        P(("cell", "section"), None),
        P(),
        P(("cell", "section"), None),
        P(),
        P("cell"),
        P("cell"),
        P("cell", None),
    )
    return jax.shard_map(
        local,
        mesh=mesh,
        in_specs=placed,
        out_specs=(P(("cell", "section"), None), P(("cell", "section"), None, None)),
        check_vma=False,
    )
```

```python
import functools

import jax
import jax.numpy as jnp
import numpy as np
from jax import lax
from jax.experimental import pallas as pl
from jax.experimental.pallas import tpu as pltpu
from jax.sharding import PartitionSpec as P

BLK = 8
THETA = 500000.0
EPS = 1e-05
ONES = 16
NEG = -1e30
VMEM_ALL = 56 * 1024 * 1024
VMEM_PART = 24 * 1024 * 1024
SMEM_SPEC = pl.BlockSpec(memory_space=pltpu.SMEM)
VMEM_SPEC = pl.BlockSpec(memory_space=pltpu.VMEM)
ANY_SPEC = pl.BlockSpec(memory_space=pl.ANY)


def rotary_tables(rows, head, spans):
    half = head // 2
    freq = THETA ** (-np.arange(half, dtype=np.float64) * 2.0 / head)
    freq = np.concatenate([freq, freq])
    inner = np.arange(rows, dtype=np.float64)[:, None] * freq
    outer = np.arange(spans, dtype=np.float64)[:, None] * rows * freq
    as32 = lambda a: jnp.asarray(a.astype(np.float32))
    return (as32(np.cos(inner)), as32(np.sin(inner)), as32(np.cos(outer)), as32(np.sin(outer)))


def own_place(prompt_ref, own_span):
    first = jnp.int32(0)
    end = jnp.int32(0)
    for p in range(prompt_ref.shape[0]):
        end = end + prompt_ref[p]
        first = jnp.where(own_span >= end, end, first)
    return first, own_span - first


def angles(depth, cos_in, sin_in, cos_out, sin_out):
    head = cos_in.shape[1]
    c0, s0 = cos_out[pl.ds(depth, 1), :], sin_out[pl.ds(depth, 1), :]
    c, s = cos_in[...], sin_in[...]
    cosine = c0 * c - s0 * s
    sine = s0 * c + c0 * s
    lane = lax.broadcasted_iota(jnp.int32, sine.shape, 1)
    return cosine, jnp.where(lane < head // 2, -sine, sine)


def rotate(x, cosine, sine):
    half = x.shape[1] // 2
    return x * cosine + jnp.concatenate([x[:, half:], x[:, :half]], axis=1) * sine


def project_kernel(plan_ref, prompt_ref, me_ref, hid_hbm, gain_ref, w_hbm, ci, si, co, so, kv_ref,
                   hid, w, scale, gain, hsem, wsem, *, group):
    rows, width = hid.shape
    head = kv_ref.shape[1] // 2
    row_tiles, k_tiles = hsem.shape[0], wsem.shape[0]
    rt, kt = rows // row_tiles, width // k_tiles
    lanes = scale.shape[1]
    hcopy = [pltpu.make_async_copy(hid_hbm.at[pl.ds(i * rt, rt)], hid.at[pl.ds(i * rt, rt)], hsem.at[i])
             for i in range(row_tiles)]
    wcopy = [pltpu.make_async_copy(w_hbm.at[pl.ds(i * kt, kt)], w.at[pl.ds(i * kt, kt)], wsem.at[i])
             for i in range(k_tiles)]
    for cp in hcopy + wcopy:
        cp.start()
    own_span = plan_ref[me_ref[0]]
    _, depth = own_place(prompt_ref, own_span)
    gain[...] = jnp.broadcast_to(gain_ref[...].astype(jnp.float32).reshape(1, width), gain.shape)

    def measure(row):
        sums = [jnp.zeros((group, lanes), jnp.float32)] * 4
        for j in range(width // lanes):
            x = hid[pl.ds(row, group), j * lanes:(j + 1) * lanes].astype(jnp.float32)
            sums[j % 4] = sums[j % 4] + x * x
        total = jnp.sum((sums[0] + sums[1]) + (sums[2] + sums[3]), axis=1, keepdims=True)
        scale[pl.ds(row, group), :] = jnp.broadcast_to(lax.rsqrt(total * (1.0 / width) + EPS), (group, lanes))

    def normalise(row):
        by = scale[pl.ds(row, group), :].reshape(group // 8, 8, lanes)
        for j in range(width // lanes):
            cols = slice(j * lanes, (j + 1) * lanes)
            x = hid[pl.ds(row, group), cols].astype(jnp.float32).reshape(group // 8, 8, lanes)
            hid[pl.ds(row, group), cols] = (x * by * gain[:, cols][None]).reshape(group, lanes).astype(jnp.bfloat16)

    for i in range(row_tiles + 1):
        if i < row_tiles:
            hcopy[i].wait()

        @pl.loop(0, rt // group)
        def _(g):
            if i < row_tiles:
                measure(pl.multiple_of(i * rt + g * group, group))
            if i > 0:
                normalise(pl.multiple_of((i - 1) * rt + g * group, group))

    cosine, sine = angles(depth, ci, si, co, so)
    for cp in wcopy:
        cp.wait()
    projected = jnp.dot(hid[...], w[...], preferred_element_type=jnp.float32)
    kv_ref[:, :head] = rotate(projected[:, :head], cosine, sine).astype(jnp.bfloat16)
    kv_ref[:, head:] = projected[:, head:].astype(jnp.bfloat16)


def project(plan, prompt_spans, me, hidden, gain, w_kv, tables):
    rows, width = hidden.shape
    row_tiles, k_tiles = 12, 4
    return pl.pallas_call(
        functools.partial(project_kernel, group=32),
        out_shape=jax.ShapeDtypeStruct((rows, w_kv.shape[1]), jnp.bfloat16),
        in_specs=[SMEM_SPEC] * 3 + [ANY_SPEC, VMEM_SPEC, ANY_SPEC] + [VMEM_SPEC] * 4,
        out_specs=VMEM_SPEC,
        scratch_shapes=[
            pltpu.VMEM((rows, width), jnp.bfloat16),
            pltpu.VMEM(w_kv.shape, jnp.bfloat16),
            pltpu.VMEM((rows, 128), jnp.float32),
            pltpu.VMEM((8, width), jnp.float32),
            pltpu.SemaphoreType.DMA((row_tiles,)),
            pltpu.SemaphoreType.DMA((k_tiles,)),
        ],
        compiler_params=pltpu.CompilerParams(vmem_limit_bytes=VMEM_ALL),
        name="project",
    )(plan, prompt_spans, me, hidden, gain, w_kv, *tables)


def softmax_step(keys, values_t, q_ref, chunk, acc, row_max, masked=None):
    count = q_ref.shape[1] // chunk
    scores, weights, factors = {}, {}, {}
    for c in range(count + 2):
        if c < count:
            cols = slice(c * chunk, (c + 1) * chunk)
            scores[c] = jnp.dot(keys, q_ref[:, cols], preferred_element_type=jnp.float32)
        if c >= 2:
            cols = slice((c - 2) * chunk, (c - 1) * chunk)
            part = jnp.dot(values_t, weights.pop(c - 2), preferred_element_type=jnp.float32)
            acc[:, cols] = acc[:, cols] * factors.pop(c - 2) + part
        if 1 <= c <= count:
            cols = slice((c - 1) * chunk, c * chunk)
            s = scores.pop(c - 1)
            if masked is not None:
                s = masked(s)
            old = row_max[:, cols]
            new = jnp.maximum(old, jnp.max(s, axis=0, keepdims=True))
            factors[c - 1] = jnp.exp(old - new)
            row_max[:, cols] = new
            weights[c - 1] = jnp.exp(s - new).astype(jnp.bfloat16)


def queries_kernel(plan_ref, prompt_ref, me_ref, place_ref, q_ref, kv_ref, ci, si, co, so,
                   qt_ref, acc, row_max, sel_ref, vt):
    rows = q_ref.shape[0]
    head = ci.shape[1]
    heads = q_ref.shape[1] // head
    me = me_ref[0]
    own_span = plan_ref[me]
    _, depth = own_place(prompt_ref, own_span)
    cosine, sine = angles(depth, ci, si, co, so)
    for h in range(heads):
        x = q_ref[:, h * head:(h + 1) * head].astype(jnp.float32)
        x = (rotate(x, cosine, sine) * head ** (-0.5)).astype(jnp.bfloat16)
        qt_ref[:, h * rows:(h + 1) * rows] = x.T
    slots = sel_ref.shape[0]
    blocks = place_ref.shape[1]
    mine = (place_ref[0:1, :] == me) & (
        place_ref[1:2, :] == lax.broadcasted_iota(jnp.int32, (slots, blocks), 0))
    block_id = lax.broadcasted_iota(jnp.int32, (slots, blocks), 1).astype(jnp.float32)
    sel_ref[...] = jnp.sum(jnp.where(mine, block_id, 0.0), axis=1, keepdims=True).astype(jnp.int32)
    acc[...] = jnp.zeros_like(acc)
    row_max[...] = jnp.full_like(row_max, NEG)
    vt[head:, :] = jnp.ones((ONES, rows), jnp.bfloat16)
    vt[:head, :] = kv_ref[:, head:].T

    def causal(s):
        key = lax.broadcasted_iota(jnp.int32, s.shape, 0)
        row = lax.broadcasted_iota(jnp.int32, s.shape, 1)
        return jnp.where(key <= row, s, NEG)

    softmax_step(kv_ref[:, :head], vt[...], qt_ref, rows, acc, row_max, causal)


def prepare(plan, prompt_spans, me, place, queries, kv, tables):
    rows = queries.shape[0]
    head = kv.shape[1] // 2
    columns = rows * (queries.shape[1] // head)
    return pl.pallas_call(
        queries_kernel,
        out_shape=(
            jax.ShapeDtypeStruct((head, columns), jnp.bfloat16),
            jax.ShapeDtypeStruct((head + ONES, columns), jnp.float32),
            jax.ShapeDtypeStruct((1, columns), jnp.float32),
            jax.ShapeDtypeStruct((rows // BLK, 1), jnp.int32),
        ),
        in_specs=[SMEM_SPEC] * 3 + [VMEM_SPEC] * 7,
        out_specs=(VMEM_SPEC,) * 4,
        scratch_shapes=[pltpu.VMEM((head + ONES, rows), jnp.bfloat16)],
        compiler_params=pltpu.CompilerParams(vmem_limit_bytes=VMEM_PART),
        name="prepare",
    )(plan, prompt_spans, me, place, queries, kv, *tables)


def taken(known, done, most, even):
    count = jnp.minimum(known - done, most)
    return count // 2 * 2 if even else count


def attend_kernel(plan_ref, prompt_ref, me_ref, src_ref, *rest, before, blocks, old, cap, even, last):
    picks = old is not None
    if picks:
        sel_ref, *rest = rest
        if before:
            goes, *rest = rest
    qt_ref, acc_in, max_in, *rest = rest
    if picks and before:
        cache_in, *rest = rest
    count = 1 + max(r for r, _ in blocks)
    refs, rest = rest[:count], rest[count:]
    if not before:
        goes, *rest = rest
    if picks:
        cache_ref, *rest = rest
    if last:
        ctx_ref, acc, row_max, kv, vt = rest
    else:
        acc, row_max, kv, vt = rest
    head, columns = qt_ref.shape
    n = plan_ref.shape[0]
    rows = kv.shape[0] // cap
    me = me_ref[0]
    own_span = plan_ref[me]
    first, _ = own_place(prompt_ref, own_span)
    spans, needed, rank = [], [], []
    seen = jnp.int32(0)
    for j in range(len(blocks)):
        span = plan_ref[src_ref[me * n + j]]
        take = (span >= first) & (span < own_span)
        spans.append(span)
        needed.append(take)
        rank.append(seen)
        seen = seen + take.astype(jnp.int32)
    rank.append(seen)
    done = jnp.int32(0)
    for arrived, most, pairs_only in before:
        done = done + taken(rank[arrived], done, most, pairs_only)
    todo = taken(seen, done, cap, even)
    for j, (operand, row) in enumerate(blocks):
        slot = rank[j] - done

        @pl.when(needed[j] & (slot >= 0) & (slot < todo))
        def _():
            kv[pl.ds(pl.multiple_of(slot * rows, rows), rows), :] = refs[operand][row:row + rows, :]

    per_span = rows // BLK
    if picks and before:
        cache_ref[...] = cache_in[...]
    elif picks:
        for i in range(2 * n):
            goes[i] = jnp.int32(-1)

        @pl.loop(0, cache_ref.shape[0], unroll=4)
        def _(slot):
            at = 2 * (sel_ref[slot, 0] // per_span)
            goes[jnp.where(goes[at] < 0, at, at + 1)] = slot

    for j in range(old if picks else len(blocks), len(blocks)):
        operand, row = blocks[j]

        @pl.when(goes[2 * spans[j]] >= 0)
        def _():
            for k in range(2):
                slot = goes[2 * spans[j] + k]
                block = sel_ref[slot, 0] - spans[j] * per_span
                start = pl.multiple_of(block // 2 * (2 * BLK), 2 * BLK)
                pair = refs[operand][pl.ds(row + start, 2 * BLK), :].astype(jnp.float32)
                cache_ref[slot] = jnp.where(block % 2 == 1, pair[BLK:], pair[:BLK]).astype(jnp.bfloat16)

    acc[...] = acc_in[...]
    row_max[...] = max_in[...]
    vt[head:, :] = jnp.ones((ONES, vt.shape[1]), jnp.bfloat16)

    def visit(slot, many):
        block = kv.at[pl.ds(pl.multiple_of(slot * rows, rows), many * rows)]
        vt[:head, :many * rows] = block[:, head:].T
        softmax_step(block[:, :head], vt[:, :many * rows], qt_ref, 512, acc, row_max)

    @pl.loop(0, todo // 2)
    def _(i):
        visit(2 * i, 2)

    if not even:
        @pl.when(todo % 2 == 1)
        def _():
            visit(todo - 1, 1)

    if last:
        for h in range(columns // rows):
            cols = slice(h * rows, (h + 1) * rows)
            out = acc[:head, cols] * (1.0 / acc[head:head + 1, cols])
            ctx_ref[:, h * head:(h + 1) * head] = out.astype(jnp.bfloat16).T


def attend(plan, prompt_spans, me, sources, sel, goes, qt, state, arrays, blocks, old, before, cap, even, rows, last):
    acc, row_max, *cache = state
    head, columns = qt.shape
    both = arrays[0].shape[1]
    n = plan.shape[0]
    scratch = [
        pltpu.VMEM((cap * rows, both), jnp.bfloat16),
        pltpu.VMEM((head + ONES, 2 * rows), jnp.bfloat16),
    ]
    carried = [jax.ShapeDtypeStruct(acc.shape, jnp.float32), jax.ShapeDtypeStruct(row_max.shape, jnp.float32)]
    picked = jax.ShapeDtypeStruct((rows // BLK, BLK, both), jnp.bfloat16)
    if last:
        out_shape = [picked, jax.ShapeDtypeStruct((rows, columns // rows * head), jnp.bfloat16)]
        scratch = [pltpu.VMEM(s.shape, s.dtype) for s in carried] + scratch
    else:
        out_shape = carried if old is None else [picked] + carried
    out_specs = [VMEM_SPEC] * len(out_shape)
    if not before:
        out_shape = [jax.ShapeDtypeStruct((2 * n,), jnp.int32)] + out_shape
        out_specs = [SMEM_SPEC] + out_specs
    scalars = [plan, prompt_spans, me, sources] + ([] if old is None else [sel] + goes)
    work = 4 * head * columns * rows * min(cap, 4)
    return pl.pallas_call(
        functools.partial(attend_kernel, before=tuple(before), blocks=tuple(blocks), old=old, cap=cap, even=even, last=last),
        out_shape=tuple(out_shape),
        in_specs=[SMEM_SPEC] * len(scalars) + [VMEM_SPEC] * (3 + len(cache) + len(arrays)),
        out_specs=tuple(out_specs),
        scratch_shapes=scratch,
        compiler_params=pltpu.CompilerParams(vmem_limit_bytes=VMEM_PART),
        cost_estimate=pl.CostEstimate(flops=2 * work, bytes_accessed=4 * 1024 * 1024, transcendentals=work // (4 * head)),
        name="finish" if last else "attend",
    )(*scalars, qt, acc, row_max, *cache, *arrays)


class Routes:
    def __init__(self, n):
        self.n = n
        self.lines = n // 8
        order = [0] + list(range(1, self.lines, 2)) + list(range(2, self.lines, 2))[::-1]
        following = {a: order[(i + 1) % self.lines] for i, a in enumerate(order)}
        preceding = {b: a for a, b in following.items()}
        self.ahead = [self.at(following[l], y, x, c) for l, y, x, c in self.all()]
        self.back = [self.at(preceding[l], y, x, c) for l, y, x, c in self.all()]
        self.flip_a = [self.at(l, y, 1 - x, c) if c == 0 else self.at(l, 1 - y, x, c) for l, y, x, c in self.all()]
        self.flip_b = [self.at(l, y, 1 - x, c) if c == 1 else self.at(l, 1 - y, x, c) for l, y, x, c in self.all()]
        self.core = [self.at(l, y, x, 1 - c) for l, y, x, c in self.all()]

    def all(self):
        return [(i // 8, (i // 4) % 2, (i // 2) % 2, i % 2) for i in range(self.n)]

    def at(self, line, y, x, core):
        return ((line * 2 + y) * 2 + x) * 2 + core


class Block:
    def __init__(self, array, sources):
        self.array, self.sources = array, sources

    def send(self, to):
        moved = []
        for source in self.sources:
            landed = [0] * len(to)
            for i, target in enumerate(to):
                landed[target] = source[i]
            moved.append(landed)
        return Block(lax.ppermute(self.array, "section", list(enumerate(to))), moved)


def join(parts):
    if len(parts) == 1:
        return parts[0]
    return Block(jnp.concatenate([p.array for p in parts], axis=0), [s for p in parts for s in p.sources])


CAPS = (4, 6, 4, 4)
PICKS = 2


def local(hidden, norm_gain, queries, w_kv, plan, prompt_spans, placement):
    n = lax.axis_size("section")
    rows = hidden.shape[0]
    head = w_kv.shape[1] // 2
    me = lax.axis_index("section").astype(jnp.int32).reshape(1)
    tables = rotary_tables(rows, head, n)
    kv = project(plan, prompt_spans, me, hidden, norm_gain, w_kv, tables)
    route = Routes(n)
    own = Block(kv, [list(range(n))])
    payload = ahead = back = own
    lines_left = route.lines - 1
    pending = []
    fresh = [own]
    arrived, before, phase = [own], [], 0
    state = qt = sel = None
    goes, cache, old = [], [], 0

    def stage(cap, even, old, last=False):
        arrays = [block.array for block in arrived]
        places = [(i, r * rows) for i, block in enumerate(arrived) for r in range(len(block.sources))]
        table = [source for block in arrived for source in block.sources]
        table = table + [[0] * n] * (n - len(table))
        sources = jnp.asarray(np.array(table, np.int32).T.reshape(-1))
        result = attend(
            plan, prompt_spans, me, sources, sel, goes, qt, state + (cache if old is not None else []), arrays, places,
            old, before, cap, even, rows, last)
        before.append((len(places), cap, even))
        return result

    while payload is not None or pending or fresh:
        crossed = [join(fresh).send(route.core)] if fresh else []
        passed = [p.send(route.flip_b) for p in pending]
        flipped, chain = [], []

        def flip():
            if payload is not None:
                b = payload.send(route.flip_b)
                flipped.extend([payload.send(route.flip_a), b])

        if phase > 0:
            ends = (lines_left > 0, lines_left > 1)
        else:
            flip()
            ends = (lines_left > 0, lines_left > 1)
        if ends[1]:
            back = back.send(route.back)
        if ends[0]:
            ahead = ahead.send(route.ahead)
        chain = ([ahead] if ends[0] else []) + ([back] if ends[1] else [])
        lines_left -= len(chain)
        if phase > 0:
            flip()
        if phase == 0:
            qt, acc, row_max, sel = prepare(plan, prompt_spans, me, placement.T, queries, kv, tables)
            state = [acc, row_max]
        else:
            picks = phase <= PICKS
            *extra, acc, row_max = stage(CAPS[min(phase - 1, len(CAPS) - 1)], phase > 1, old if picks else None)
            state = [acc, row_max]
            if picks:
                *listed, cache_now = extra
                goes, cache, old = listed or goes, [cache_now], before[-1][0]
        everything = crossed + passed + (flipped + chain if phase == 0 else chain + flipped)
        held, state = lax.optimization_barrier(([block.array for block in everything], state))
        for block, array in zip(everything, held):
            block.array = array
        payload = join(chain) if chain else None
        pending = flipped[:1]
        if len(chain) > 1:
            waiting = [payload] + chain + pending
            held = lax.optimization_barrier([block.array for block in waiting])
            for block, array in zip(waiting, held):
                block.array = array
        fresh = ([payload] if payload is not None else []) + flipped + passed
        arrived = arrived + crossed + fresh
        phase += 1
    cache_out, context = stage(n, False, old, True)
    return context, cache_out


def solution(mesh):
    placed = (
        P(("cell", "section"), None),
        P(),
        P(("cell", "section"), None),
        P(),
        P("cell"),
        P("cell"),
        P("cell", None),
    )
    return jax.shard_map(
        local,
        mesh=mesh,
        in_specs=placed,
        out_specs=(P(("cell", "section"), None), P(("cell", "section"), None, None)),
        check_vma=False,
    )
```

```python
import functools

import jax
import jax.numpy as jnp
import numpy as np
from jax import lax
from jax.experimental import pallas as pl
from jax.experimental.pallas import tpu as pltpu
from jax.sharding import PartitionSpec as P

BLK = 8
THETA = 500000.0
EPS = 1e-05
ONES = 16
NEG = -1e30
VMEM_ALL = 56 * 1024 * 1024
VMEM_PART = 24 * 1024 * 1024
SMEM_SPEC = pl.BlockSpec(memory_space=pltpu.SMEM)
VMEM_SPEC = pl.BlockSpec(memory_space=pltpu.VMEM)
ANY_SPEC = pl.BlockSpec(memory_space=pl.ANY)


def rotary_tables(rows, head, spans):
    half = head // 2
    freq = THETA ** (-np.arange(half, dtype=np.float64) * 2.0 / head)
    freq = np.concatenate([freq, freq])
    inner = np.arange(rows, dtype=np.float64)[:, None] * freq
    outer = np.arange(spans, dtype=np.float64)[:, None] * rows * freq
    as32 = lambda a: jnp.asarray(a.astype(np.float32))
    return (as32(np.cos(inner)), as32(np.sin(inner)), as32(np.cos(outer)), as32(np.sin(outer)))


def own_place(prompt_ref, own_span):
    first = jnp.int32(0)
    end = jnp.int32(0)
    for p in range(prompt_ref.shape[0]):
        end = end + prompt_ref[p]
        first = jnp.where(own_span >= end, end, first)
    return first, own_span - first


def angles(depth, cos_in, sin_in, cos_out, sin_out):
    head = cos_in.shape[1]
    c0, s0 = cos_out[pl.ds(depth, 1), :], sin_out[pl.ds(depth, 1), :]
    c, s = cos_in[...], sin_in[...]
    cosine = c0 * c - s0 * s
    sine = s0 * c + c0 * s
    lane = lax.broadcasted_iota(jnp.int32, sine.shape, 1)
    return cosine, jnp.where(lane < head // 2, -sine, sine)


def rotate(x, cosine, sine):
    half = x.shape[1] // 2
    return x * cosine + jnp.concatenate([x[:, half:], x[:, :half]], axis=1) * sine


def project_kernel(plan_ref, prompt_ref, me_ref, hid_hbm, gain_ref, w_hbm, ci, si, co, so, kv_ref,
                   hid, w, scale, gain, hsem, wsem, *, group):
    rows, width = hid.shape
    head = kv_ref.shape[1] // 2
    row_tiles, k_tiles = hsem.shape[0], wsem.shape[0]
    rt, kt = rows // row_tiles, width // k_tiles
    lanes = scale.shape[1]
    hcopy = [pltpu.make_async_copy(hid_hbm.at[pl.ds(i * rt, rt)], hid.at[pl.ds(i * rt, rt)], hsem.at[i])
             for i in range(row_tiles)]
    wcopy = [pltpu.make_async_copy(w_hbm.at[pl.ds(i * kt, kt)], w.at[pl.ds(i * kt, kt)], wsem.at[i])
             for i in range(k_tiles)]
    for cp in hcopy + wcopy:
        cp.start()
    own_span = plan_ref[me_ref[0]]
    _, depth = own_place(prompt_ref, own_span)
    gain[...] = jnp.broadcast_to(gain_ref[...].astype(jnp.float32).reshape(1, width), gain.shape)

    def measure(row):
        sums = [jnp.zeros((group, lanes), jnp.float32)] * 4
        for j in range(width // lanes):
            x = hid[pl.ds(row, group), j * lanes:(j + 1) * lanes].astype(jnp.float32)
            sums[j % 4] = sums[j % 4] + x * x
        total = jnp.sum((sums[0] + sums[1]) + (sums[2] + sums[3]), axis=1, keepdims=True)
        scale[pl.ds(row, group), :] = jnp.broadcast_to(lax.rsqrt(total * (1.0 / width) + EPS), (group, lanes))

    def normalise(row):
        by = scale[pl.ds(row, group), :].reshape(group // 8, 8, lanes)
        for j in range(width // lanes):
            cols = slice(j * lanes, (j + 1) * lanes)
            x = hid[pl.ds(row, group), cols].astype(jnp.float32).reshape(group // 8, 8, lanes)
            hid[pl.ds(row, group), cols] = (x * by * gain[:, cols][None]).reshape(group, lanes).astype(jnp.bfloat16)

    for i in range(row_tiles + 1):
        if i < row_tiles:
            hcopy[i].wait()

        @pl.loop(0, rt // group)
        def _(g):
            if i < row_tiles:
                measure(pl.multiple_of(i * rt + g * group, group))
            if i > 0:
                normalise(pl.multiple_of((i - 1) * rt + g * group, group))

    cosine, sine = angles(depth, ci, si, co, so)
    for cp in wcopy:
        cp.wait()
    projected = jnp.dot(hid[...], w[...], preferred_element_type=jnp.float32)
    kv_ref[:, :head] = rotate(projected[:, :head], cosine, sine).astype(jnp.bfloat16)
    kv_ref[:, head:] = projected[:, head:].astype(jnp.bfloat16)


def project(plan, prompt_spans, me, hidden, gain, w_kv, tables):
    rows, width = hidden.shape
    row_tiles, k_tiles = 12, 4
    return pl.pallas_call(
        functools.partial(project_kernel, group=32),
        out_shape=jax.ShapeDtypeStruct((rows, w_kv.shape[1]), jnp.bfloat16),
        in_specs=[SMEM_SPEC] * 3 + [ANY_SPEC, VMEM_SPEC, ANY_SPEC] + [VMEM_SPEC] * 4,
        out_specs=VMEM_SPEC,
        scratch_shapes=[
            pltpu.VMEM((rows, width), jnp.bfloat16),
            pltpu.VMEM(w_kv.shape, jnp.bfloat16),
            pltpu.VMEM((rows, 128), jnp.float32),
            pltpu.VMEM((8, width), jnp.float32),
            pltpu.SemaphoreType.DMA((row_tiles,)),
            pltpu.SemaphoreType.DMA((k_tiles,)),
        ],
        compiler_params=pltpu.CompilerParams(vmem_limit_bytes=VMEM_ALL),
        name="project",
    )(plan, prompt_spans, me, hidden, gain, w_kv, *tables)


def softmax_step(keys, values_t, q_ref, chunk, acc, row_max, masked=None):
    count = q_ref.shape[1] // chunk
    scores, weights, factors = {}, {}, {}
    for c in range(count + 2):
        if c < count:
            cols = slice(c * chunk, (c + 1) * chunk)
            scores[c] = jnp.dot(keys, q_ref[:, cols], preferred_element_type=jnp.float32)
        if c >= 2:
            cols = slice((c - 2) * chunk, (c - 1) * chunk)
            part = jnp.dot(values_t, weights.pop(c - 2), preferred_element_type=jnp.float32)
            acc[:, cols] = acc[:, cols] * factors.pop(c - 2) + part
        if 1 <= c <= count:
            cols = slice((c - 1) * chunk, c * chunk)
            s = scores.pop(c - 1)
            if masked is not None:
                s = masked(s)
            old = row_max[:, cols]
            new = jnp.maximum(old, jnp.max(s, axis=0, keepdims=True))
            factors[c - 1] = jnp.exp(old - new)
            row_max[:, cols] = new
            weights[c - 1] = jnp.exp(s - new).astype(jnp.bfloat16)


def queries_kernel(plan_ref, prompt_ref, me_ref, place_ref, q_ref, kv_ref, ci, si, co, so,
                   qt_ref, acc, row_max, sel_ref, vt):
    rows = q_ref.shape[0]
    head = ci.shape[1]
    heads = q_ref.shape[1] // head
    me = me_ref[0]
    own_span = plan_ref[me]
    _, depth = own_place(prompt_ref, own_span)
    cosine, sine = angles(depth, ci, si, co, so)
    for h in range(heads):
        x = q_ref[:, h * head:(h + 1) * head].astype(jnp.float32)
        x = (rotate(x, cosine, sine) * head ** (-0.5)).astype(jnp.bfloat16)
        qt_ref[:, h * rows:(h + 1) * rows] = x.T
    slots = sel_ref.shape[0]
    blocks = place_ref.shape[1]
    mine = (place_ref[0:1, :] == me) & (
        place_ref[1:2, :] == lax.broadcasted_iota(jnp.int32, (slots, blocks), 0))
    block_id = lax.broadcasted_iota(jnp.int32, (slots, blocks), 1).astype(jnp.float32)
    sel_ref[...] = jnp.sum(jnp.where(mine, block_id, 0.0), axis=1, keepdims=True).astype(jnp.int32)
    acc[...] = jnp.zeros_like(acc)
    row_max[...] = jnp.full_like(row_max, NEG)
    vt[head:, :] = jnp.ones((ONES, rows), jnp.bfloat16)
    vt[:head, :] = kv_ref[:, head:].T

    def causal(s):
        key = lax.broadcasted_iota(jnp.int32, s.shape, 0)
        row = lax.broadcasted_iota(jnp.int32, s.shape, 1)
        return jnp.where(key <= row, s, NEG)

    softmax_step(kv_ref[:, :head], vt[...], qt_ref, rows, acc, row_max, causal)


def prepare(plan, prompt_spans, me, place, queries, kv, tables):
    rows = queries.shape[0]
    head = kv.shape[1] // 2
    columns = rows * (queries.shape[1] // head)
    return pl.pallas_call(
        queries_kernel,
        out_shape=(
            jax.ShapeDtypeStruct((head, columns), jnp.bfloat16),
            jax.ShapeDtypeStruct((head + ONES, columns), jnp.float32),
            jax.ShapeDtypeStruct((1, columns), jnp.float32),
            jax.ShapeDtypeStruct((rows // BLK, 1), jnp.int32),
        ),
        in_specs=[SMEM_SPEC] * 3 + [VMEM_SPEC] * 7,
        out_specs=(VMEM_SPEC,) * 4,
        scratch_shapes=[pltpu.VMEM((head + ONES, rows), jnp.bfloat16)],
        compiler_params=pltpu.CompilerParams(vmem_limit_bytes=VMEM_PART),
        name="prepare",
    )(plan, prompt_spans, me, place, queries, kv, *tables)


def taken(known, done, most, even):
    count = jnp.minimum(known - done, most)
    return count // 2 * 2 if even else count


def attend_kernel(plan_ref, prompt_ref, me_ref, src_ref, *rest, before, blocks, old, cap, even, last):
    picks = old is not None
    if picks:
        sel_ref, *rest = rest
        if before:
            goes, *rest = rest
    qt_ref, acc_in, max_in, *rest = rest
    if picks and before:
        cache_in, *rest = rest
    count = 1 + max(r for r, _ in blocks)
    refs, rest = rest[:count], rest[count:]
    if not before:
        goes, *rest = rest
    if picks:
        cache_ref, *rest = rest
    if last:
        ctx_hbm, acc, row_max, kv, vt, ctx_ref, ctx_sem = rest
    else:
        acc, row_max, kv, vt = rest
    head, columns = qt_ref.shape
    n = plan_ref.shape[0]
    rows = kv.shape[0] // cap
    me = me_ref[0]
    own_span = plan_ref[me]
    first, _ = own_place(prompt_ref, own_span)
    spans, needed, rank = [], [], []
    seen = jnp.int32(0)
    for j in range(len(blocks)):
        span = plan_ref[src_ref[me * n + j]]
        take = (span >= first) & (span < own_span)
        spans.append(span)
        needed.append(take)
        rank.append(seen)
        seen = seen + take.astype(jnp.int32)
    rank.append(seen)
    done = jnp.int32(0)
    for arrived, most, pairs_only in before:
        done = done + taken(rank[arrived], done, most, pairs_only)
    todo = taken(seen, done, cap, even)
    for j, (operand, row) in enumerate(blocks):
        slot = rank[j] - done

        @pl.when(needed[j] & (slot >= 0) & (slot < todo))
        def _():
            kv[pl.ds(pl.multiple_of(slot * rows, rows), rows), :] = refs[operand][row:row + rows, :]

    per_span = rows // BLK
    if picks and before:
        cache_ref[...] = cache_in[...]
    elif picks:
        for i in range(2 * n):
            goes[i] = jnp.int32(-1)

        @pl.loop(0, cache_ref.shape[0], unroll=4)
        def _(slot):
            at = 2 * (sel_ref[slot, 0] // per_span)
            goes[jnp.where(goes[at] < 0, at, at + 1)] = slot

    for j in range(old if picks else len(blocks), len(blocks)):
        operand, row = blocks[j]

        @pl.when(goes[2 * spans[j]] >= 0)
        def _():
            for k in range(2):
                slot = goes[2 * spans[j] + k]
                block = sel_ref[slot, 0] - spans[j] * per_span
                start = pl.multiple_of(block // 2 * (2 * BLK), 2 * BLK)
                pair = refs[operand][pl.ds(row + start, 2 * BLK), :].astype(jnp.float32)
                cache_ref[slot] = jnp.where(block % 2 == 1, pair[BLK:], pair[:BLK]).astype(jnp.bfloat16)

    acc[...] = acc_in[...]
    row_max[...] = max_in[...]
    vt[head:, :] = jnp.ones((ONES, vt.shape[1]), jnp.bfloat16)

    def visit(slot, many):
        block = kv.at[pl.ds(pl.multiple_of(slot * rows, rows), many * rows)]
        vt[:head, :many * rows] = block[:, head:].T
        softmax_step(block[:, :head], vt[:, :many * rows], qt_ref, 512, acc, row_max)

    @pl.loop(0, todo // 2)
    def _(i):
        visit(2 * i, 2)

    if not even:
        @pl.when(todo % 2 == 1)
        def _():
            visit(todo - 1, 1)

    if last:
        leaving = []
        for h in range(columns // rows):
            cols = slice(h * rows, (h + 1) * rows)
            out = acc[:head, cols] * (1.0 / acc[head:head + 1, cols])
            wide = slice(h * head, (h + 1) * head)
            ctx_ref[:, wide] = out.astype(jnp.bfloat16).T
            leave = pltpu.make_async_copy(ctx_ref.at[:, wide], ctx_hbm.at[:, wide], ctx_sem.at[h])
            leave.start()
            leaving.append(leave)
        for leave in leaving:
            leave.wait()


def attend(plan, prompt_spans, me, sources, sel, goes, qt, state, arrays, blocks, old, before, cap, even, rows, last):
    acc, row_max, *cache = state
    head, columns = qt.shape
    both = arrays[0].shape[1]
    n = plan.shape[0]
    scratch = [
        pltpu.VMEM((cap * rows, both), jnp.bfloat16),
        pltpu.VMEM((head + ONES, 2 * rows), jnp.bfloat16),
    ]
    carried = [jax.ShapeDtypeStruct(acc.shape, jnp.float32), jax.ShapeDtypeStruct(row_max.shape, jnp.float32)]
    picked = jax.ShapeDtypeStruct((rows // BLK, BLK, both), jnp.bfloat16)
    if last:
        out_shape = [picked, jax.ShapeDtypeStruct((rows, columns // rows * head), jnp.bfloat16)]
        scratch = [pltpu.VMEM(s.shape, s.dtype) for s in carried] + scratch
        scratch += [pltpu.VMEM(out_shape[1].shape, jnp.bfloat16), pltpu.SemaphoreType.DMA((columns // rows,))]
    else:
        out_shape = carried if old is None else [picked] + carried
    out_specs = [VMEM_SPEC] * len(out_shape)
    if last:
        out_specs[1] = ANY_SPEC
    if not before:
        out_shape = [jax.ShapeDtypeStruct((2 * n,), jnp.int32)] + out_shape
        out_specs = [SMEM_SPEC] + out_specs
    scalars = [plan, prompt_spans, me, sources] + ([] if old is None else [sel] + goes)
    work = 4 * head * columns * rows * min(cap, 4)
    return pl.pallas_call(
        functools.partial(attend_kernel, before=tuple(before), blocks=tuple(blocks), old=old, cap=cap, even=even, last=last),
        out_shape=tuple(out_shape),
        in_specs=[SMEM_SPEC] * len(scalars) + [VMEM_SPEC] * (3 + len(cache) + len(arrays)),
        out_specs=tuple(out_specs),
        scratch_shapes=scratch,
        compiler_params=pltpu.CompilerParams(vmem_limit_bytes=VMEM_PART),
        cost_estimate=pl.CostEstimate(flops=2 * work, bytes_accessed=4 * 1024 * 1024, transcendentals=work // (4 * head)),
        name="finish" if last else "attend",
    )(*scalars, qt, acc, row_max, *cache, *arrays)


class Routes:
    def __init__(self, n):
        self.n = n
        self.lines = n // 8
        order = [0] + list(range(1, self.lines, 2)) + list(range(2, self.lines, 2))[::-1]
        following = {a: order[(i + 1) % self.lines] for i, a in enumerate(order)}
        preceding = {b: a for a, b in following.items()}
        self.ahead = [self.at(following[l], y, x, c) for l, y, x, c in self.all()]
        self.back = [self.at(preceding[l], y, x, c) for l, y, x, c in self.all()]
        self.flip_a = [self.at(l, y, 1 - x, c) if c == 0 else self.at(l, 1 - y, x, c) for l, y, x, c in self.all()]
        self.flip_b = [self.at(l, y, 1 - x, c) if c == 1 else self.at(l, 1 - y, x, c) for l, y, x, c in self.all()]
        self.core = [self.at(l, y, x, 1 - c) for l, y, x, c in self.all()]

    def all(self):
        return [(i // 8, (i // 4) % 2, (i // 2) % 2, i % 2) for i in range(self.n)]

    def at(self, line, y, x, core):
        return ((line * 2 + y) * 2 + x) * 2 + core


class Block:
    def __init__(self, array, sources):
        self.array, self.sources = array, sources

    def send(self, to):
        moved = []
        for source in self.sources:
            landed = [0] * len(to)
            for i, target in enumerate(to):
                landed[target] = source[i]
            moved.append(landed)
        return Block(lax.ppermute(self.array, "section", list(enumerate(to))), moved)


def join(parts):
    if len(parts) == 1:
        return parts[0]
    return Block(jnp.concatenate([p.array for p in parts], axis=0), [s for p in parts for s in p.sources])


CAPS = (4, 6, 4, 4)
PICKS = 2


def local(hidden, norm_gain, queries, w_kv, plan, prompt_spans, placement):
    n = lax.axis_size("section")
    rows = hidden.shape[0]
    head = w_kv.shape[1] // 2
    me = lax.axis_index("section").astype(jnp.int32).reshape(1)
    tables = rotary_tables(rows, head, n)
    kv = project(plan, prompt_spans, me, hidden, norm_gain, w_kv, tables)
    route = Routes(n)
    own = Block(kv, [list(range(n))])
    payload = ahead = back = own
    lines_left = route.lines - 1
    pending = []
    fresh = [own]
    arrived, before, phase = [own], [], 0
    state = qt = sel = None
    goes, cache, old = [], [], 0

    def stage(cap, even, old, last=False):
        arrays = [block.array for block in arrived]
        places = [(i, r * rows) for i, block in enumerate(arrived) for r in range(len(block.sources))]
        table = [source for block in arrived for source in block.sources]
        table = table + [[0] * n] * (n - len(table))
        sources = jnp.asarray(np.array(table, np.int32).T.reshape(-1))
        result = attend(
            plan, prompt_spans, me, sources, sel, goes, qt, state + (cache if old is not None else []), arrays, places,
            old, before, cap, even, rows, last)
        before.append((len(places), cap, even))
        return result

    while payload is not None or pending or fresh:
        crossed = [join(fresh).send(route.core)] if fresh else []
        passed = [p.send(route.flip_b) for p in pending]
        flipped, chain = [], []

        def flip():
            if payload is not None:
                b = payload.send(route.flip_b)
                flipped.extend([payload.send(route.flip_a), b])

        if phase > 0:
            ends = (lines_left > 0, lines_left > 1)
        else:
            flip()
            ends = (lines_left > 0, lines_left > 1)
        if ends[1]:
            back = back.send(route.back)
        if ends[0]:
            ahead = ahead.send(route.ahead)
        chain = ([ahead] if ends[0] else []) + ([back] if ends[1] else [])
        lines_left -= len(chain)
        if phase > 0:
            flip()
        if phase == 0:
            qt, acc, row_max, sel = prepare(plan, prompt_spans, me, placement.T, queries, kv, tables)
            state = [acc, row_max]
        else:
            picks = phase <= PICKS
            *extra, acc, row_max = stage(CAPS[min(phase - 1, len(CAPS) - 1)], phase > 1, old if picks else None)
            state = [acc, row_max]
            if picks:
                *listed, cache_now = extra
                goes, cache, old = listed or goes, [cache_now], before[-1][0]
        everything = crossed + passed + (flipped + chain if phase == 0 else chain + flipped)
        held, state = lax.optimization_barrier(([block.array for block in everything], state))
        for block, array in zip(everything, held):
            block.array = array
        payload = join(chain) if chain else None
        pending = flipped[:1]
        if len(chain) > 1:
            waiting = [payload] + chain + pending
            held = lax.optimization_barrier([block.array for block in waiting])
            for block, array in zip(waiting, held):
                block.array = array
        fresh = ([payload] if payload is not None else []) + flipped + passed
        arrived = arrived + crossed + fresh
        phase += 1
    cache_out, context = stage(n, False, old, True)
    return context, cache_out


def solution(mesh):
    placed = (
        P(("cell", "section"), None),
        P(),
        P(("cell", "section"), None),
        P(),
        P("cell"),
        P("cell"),
        P("cell", None),
    )
    return jax.shard_map(
        local,
        mesh=mesh,
        in_specs=placed,
        out_specs=(P(("cell", "section"), None), P(("cell", "section"), None, None)),
        check_vma=False,
    )
```
